128 devices in a mesh: fsdp: 64 (over x_hi, z, y, core), seq: 2 (over x_lo).
Axes of the slice: x: 4 (x_hi: 2, x_lo: 2; x = x_hi * 2 + x_lo), y: 4, z: 4, core: 2. Of those that a mesh axis runs over, the one named last changes fastest.
Arguments:
- hidden_in: bfloat16 [64, 256, 2048], P('fsdp', 'seq'), may hold values from -6 to 6
- norm_gain: bfloat16 [2048], P('fsdp'), may hold values from 0.099609375 to 1.8984375
- norm_shift: bfloat16 [2048], P('fsdp'), may hold values from -4 to 4
- qkv_weight: bfloat16 [2048, 6144], P('fsdp'), may hold values from -0.125 to 0.125
- qkv_bias: bfloat16 [6144], P('fsdp'), may hold values from -4 to 4
- proj_weight: bfloat16 [2048, 2048], P('fsdp'), may hold values from -0.5 to 0.5
- proj_bias: bfloat16 [2048], P('fsdp'), may hold values from -4 to 4
- up_weight: bfloat16 [2048, 8192], P('fsdp'), may hold values from -0.125 to 0.125
- up_bias: bfloat16 [8192], P('fsdp'), may hold values from -6 to 6
- down_weight: bfloat16 [8192, 2048], P('fsdp'), may hold values from -0.0625 to 0.0625
- down_bias: bfloat16 [2048], P('fsdp'), may hold values from -4 to 4
- segment_ids: int32 [64, 256], P('fsdp'), may hold values from 0 to 2, as said below
- positions: int32 [64, 256], P('fsdp', 'seq'), may hold values from 0 to 1023, as said below
- cotangent: bfloat16 [64, 256, 2048], P('fsdp', 'seq'), may hold values from -16 to 16
Outputs:
- block_out: bfloat16 [64, 256, 2048], P('fsdp', 'seq')
- grad_hidden: float32 [64, 256, 2048], P('fsdp', 'seq')
- grad_gain: float32 [2048], P('fsdp')
- grad_shift: float32 [2048], P('fsdp')
- grad_qkv: float32 [2048, 6144], P('fsdp')
- grad_qkv_bias: float32 [6144], P('fsdp')
- grad_proj: float32 [2048, 2048], P('fsdp')
- grad_proj_bias: float32 [2048], P('fsdp')
- grad_up: float32 [2048, 8192], P('fsdp')
- grad_up_bias: float32 [8192], P('fsdp')
- grad_down: float32 [8192, 2048], P('fsdp')
- grad_down_bias: float32 [2048], P('fsdp')
The draws below stay inside these ranges and needn't reach their ends.
Inputs may be any that keep to these rules, and one draw needn't show every extreme that they name: `segment_ids`: ids never fall along a sequence; every sequence holds three documents, ids 0, 1 and 2; the first and the last have 256/8 to 95 tokens. `positions`: within a document the position rises by one from token to token; the first document of a sequence starts at 0; the last token of every sequence has the largest position.
All inputs are finite; a program needn't handle non-finite values.
Results may differ from the reference program's by a relative error of at most 0.009.
Values may be sent and summed in bfloat16 or wider, within the bound.
No kernel may reach another device: no remote copies, remote signals or barrier semaphores. Data moves between devices by JAX's collectives and lax.ppermute only.
A program may use at most 896 MiB of HBM per device.

```python
import math
import jax
import jax.numpy as jnp
from jax import lax

D = 2048
H = 32
HD = 64
ROT = 32
FF = 8192
SEQ = 256
SEQS = 64


def document_cuts(key):
    eighth = SEQ // 8
    first_key, second_key = jax.random.split(key)
    first = jax.random.randint(first_key, (SEQS,), eighth, SEQ // 2 - eighth)
    second = jax.random.randint(second_key, (SEQS,), SEQ // 2 + eighth + 1, SEQ - eighth + 1)
    return (first, second)


def draw_segment_ids(key, part):
    first, second = document_cuts(key)
    order = jnp.arange(SEQ)[None, :]
    above_first = (order >= first[:, None]).astype(jnp.int32)
    above_second = (order >= second[:, None]).astype(jnp.int32)
    return above_first + above_second


def draw_positions(key, part):
    first, second = document_cuts(key)
    key = jax.random.fold_in(key, 5)
    final = max(1023, SEQ - 1)
    middle_len = second - first
    middle_start = jax.random.randint(key, (SEQS,), 0, final + 2 - middle_len)
    last_start = final + 1 - (SEQ - second)
    order = jnp.arange(SEQ)[None, :]
    first_cut = first[:, None]
    second_cut = second[:, None]
    middle = order - first_cut + middle_start[:, None]
    last = order - second_cut + last_start[:, None]
    inner = jnp.where(order < second_cut, middle, last)
    return jnp.where(order < first_cut, order, inner).astype(jnp.int32)


def strengthened(result, rng, source, target, shards_of, factor):
    owner, partner = [(jnp.arange(result.shape[dim]) // (result.shape[dim] // shards_of)).reshape([-1 if axis == dim else 1 for axis in range(result.ndim)]) for dim in (source, target)]
    chosen = jax.random.permutation(rng, shards_of)[partner]
    strong = (owner == chosen) | (owner == (partner + shards_of // 2) % shards_of)
    return jnp.where(strong, factor * result, result)


def block_scale(rng, shape, pieces, low, largest):
    loudness, own = 1.0, jax.random.fold_in(rng, 6)
    for dim, parts in pieces:
        draws = jnp.exp(jax.random.uniform(jax.random.fold_in(own, dim), (parts,), jnp.float32, low / len(pieces), largest / len(pieces)))
        loudness = loudness * jnp.repeat(draws, shape[dim] // parts).reshape([-1 if axis == dim else 1 for axis in range(len(shape))])
    return loudness


def noise(own_key, extent, deviation, limit, pieces=(), held_as=jnp.bfloat16):
    entries = jax.random.normal(own_key, extent, jnp.float32) * deviation
    if len(pieces) > 0:
        entries = block_scale(own_key, extent, pieces, -0.22, 0.18) * entries
    return jnp.clip(entries, min=-limit, max=limit).astype(held_as)


def heavy_noise(key, dims, width, reach, pieces, heavy, kind=jnp.bfloat16):
    values = width * jax.random.normal(key, dims, jnp.float32)
    if pieces:
        values = values * block_scale(key, dims, pieces, -0.22, 0.18)
    return jnp.clip(strengthened(values, jax.random.fold_in(key, 3), *heavy), -reach, reach).astype(kind)


def setup_inputs(seed: int = 0) -> dict:
    seeds = jax.random.split(jax.random.key(seed), 15)
    hidden_in = noise(seeds[0], (SEQS, SEQ, D), 1.0, 6.0, ((0, 64), (1, 2)))
    norm_gain = jnp.clip(1.0 + 0.18 * jax.random.normal(seeds[1], (D,), jnp.float32), 0.099609375, 1.8984375).astype(jnp.bfloat16)
    norm_shift = noise(seeds[2], (D,), 0.3, 4.0, ((0, 64),))
    qkv_weight = noise(seeds[3], (D, 3 * D), D ** -0.5, 0.125, ((0, 64),))
    qkv_bias = noise(seeds[4], (3 * D,), 0.3, 4.0, ((0, 64),))
    proj_weight = noise(seeds[5], (D, D), (D // 16) ** -0.5, 0.5, ((0, 64),))
    proj_bias = noise(seeds[6], (D,), 0.3, 4.0, ((0, 64),))
    up_weight = noise(seeds[7], (D, FF), D ** -0.5, 0.125, ((0, 64),))
    up_bias = noise(seeds[8], (FF,), 0.5, 6.0, ((0, 64),))
    down_weight = noise(seeds[9], (FF, D), FF ** -0.5, 0.0625, ((0, 64),))
    down_bias = noise(seeds[10], (D,), 0.3, 4.0, ((0, 64),))
    segment_ids = draw_segment_ids(jax.random.fold_in(seeds[14], 71), 0)
    positions = draw_positions(jax.random.fold_in(seeds[14], 71), 0)
    cotangent = heavy_noise(seeds[13], (SEQS, SEQ, D), 1.0, 16.0, ((0, 64), (1, 2)), (0, 2, 64, 4.0))
    return dict(hidden_in=hidden_in, norm_gain=norm_gain, norm_shift=norm_shift, qkv_weight=qkv_weight, qkv_bias=qkv_bias, proj_weight=proj_weight, proj_bias=proj_bias, up_weight=up_weight, up_bias=up_bias, down_weight=down_weight, down_bias=down_bias, segment_ids=segment_ids, positions=positions, cotangent=cotangent)


@jax.custom_vjp
def low(v):
    return lax.optimization_barrier(v.astype(jnp.bfloat16)).astype(jnp.float32)

@jax.custom_vjp
def low_back(v):
    return v

def low_keep(v):
    return (low(v), None)

def low_pass(kept, grad):
    return (grad,)

def back_keep(v):
    return (v, None)

def back_low(kept, grad):
    return (low(grad),)
low.defvjp(low_keep, low_pass)
low_back.defvjp(back_keep, back_low)
norm_eps = 1e-05
highest = lax.Precision.HIGHEST

def rotary(values, position):
    half_rot = ROT // 2
    freqs = 10000.0 ** (-jnp.arange(half_rot, dtype=jnp.float32) * (2.0 / ROT))
    angles = position.astype(jnp.float32)[..., None] * freqs
    cosine = jnp.cos(angles)[..., None, :]
    sine = jnp.sin(angles)[..., None, :]
    first = values[..., :half_rot]
    second = values[..., half_rot:ROT]
    rest = values[..., ROT:]
    return jnp.concatenate([first * cosine - second * sine, second * cosine + first * sine, rest], axis=-1)

def attend(query, keys, values, segment):
    scale = 1.0 / math.sqrt(HD)
    raw = jnp.einsum('qhd,khd->hqk', query, keys, precision=highest)
    scores = low_back(scale * raw)
    order = jnp.arange(segment.shape[0])
    allowed = (order[None, :] <= order[:, None]) & (segment[None, :] == segment[:, None])
    scores = jnp.where(allowed[None], scores, -1e+30)
    top = lax.optimization_barrier(jnp.max(scores, axis=-1, keepdims=True))
    expo = jnp.exp(scores - top)
    probs = low(expo / lax.optimization_barrier(jnp.sum(expo, axis=-1, keepdims=True)))
    return jnp.einsum('hqk,khd->qhd', probs, values, precision=highest)

def layer(hidden, gain, shift, qkv_w, qkv_b, proj_w, proj_b, up_w, up_b, down_w, down_b, segment, position):
    count, length = (hidden.shape[0], hidden.shape[1])
    mean = lax.optimization_barrier(jnp.mean(hidden, axis=-1, keepdims=True))
    centered = hidden - mean
    spread = lax.optimization_barrier(jnp.mean(centered * centered, axis=-1, keepdims=True))
    normal = centered * lax.rsqrt(spread + norm_eps)
    normed = low(normal * gain + shift)
    merged = low_back(jnp.einsum('nsd,de->nse', normed, qkv_w, precision=highest) + qkv_b)
    query = merged[..., :D].reshape(count, length, H, HD)
    keys = merged[..., D:2 * D].reshape(count, length, H, HD)
    values = low(merged[..., 2 * D:].reshape(count, length, H, HD))
    query = low(rotary(query, position))
    keys = low(rotary(keys, position))
    context = lax.map(lambda item: jax.checkpoint(attend)(*item), (query, keys, values, segment))
    context = low(low_back(context.reshape(count, length, D)))
    upper = low_back(jnp.einsum('nsd,df->nsf', normed, up_w, precision=highest) + up_b)
    active = low(jax.nn.gelu(upper, approximate=True))
    branch = jnp.einsum('nsd,de->nse', context, proj_w, precision=highest)
    branch = branch + jnp.einsum('nsf,fe->nse', active, down_w, precision=highest)
    return hidden + branch + proj_b + down_b

def reference(hidden_in, norm_gain, norm_shift, qkv_weight, qkv_bias, proj_weight, proj_bias, up_weight, up_bias, down_weight, down_bias, segment_ids, positions, cotangent):
    params = tuple((item.astype(jnp.float32) for item in (norm_gain, norm_shift, qkv_weight, qkv_bias, proj_weight, proj_bias, up_weight, up_bias, down_weight, down_bias)))
    total_seqs = hidden_in.shape[0]
    per_group = max([1] + [c for c in range(1, total_seqs + 1) if total_seqs % c == 0 and c * SEQ <= 4096])
    groups = total_seqs // per_group
    hidden = hidden_in.astype(jnp.float32).reshape(groups, per_group, SEQ, D)
    grad_in = cotangent.astype(jnp.float32).reshape(groups, per_group, SEQ, D)
    segment = segment_ids.reshape(groups, per_group, SEQ)
    position = positions.reshape(groups, per_group, SEQ)

    def one_group(totals, item):
        block, grad_block, seg_block, pos_block = item

        def apply(block_in, *weights):
            return layer(block_in, *weights, seg_block, pos_block)
        output, pullback = jax.vjp(apply, block, *params)
        grads = pullback(grad_block)
        totals = tuple((t + g for t, g in zip(totals, grads[1:])))
        return (totals, (output.astype(jnp.bfloat16), grads[0]))
    zeros = tuple((jnp.zeros_like(item) for item in params))
    totals, (outputs, grad_hidden) = lax.scan(one_group, zeros, (hidden, grad_in, segment, position))
    block_out = outputs.reshape(total_seqs, SEQ, D)
    grad_hidden = grad_hidden.reshape(total_seqs, SEQ, D)
    return (block_out, grad_hidden, totals[0], totals[1], totals[2], totals[3], totals[4], totals[5], totals[6], totals[7], totals[8], totals[9])
```

```python
import math

import jax
import jax.numpy as jnp
from jax import lax
from jax.experimental import pallas as pl
from jax.experimental.pallas import tpu as pltpu
from jax.sharding import Mesh, PartitionSpec as P

D = 2048
H = 32
HD = 64
ROT = 32
FF = 8192
SEQ = 256
SCALE = HD**-0.5
EPS = 1e-5
AXES = ("xh", "z", "y", "core", "xl")
SHARD = ("xh", "z", "y", "core")
PLANE = ("z", "y")
GROUP = ("xh", "core", "xl")
TOKENS = 1024
BF = jnp.bfloat16
F32 = jnp.float32


def swap(value, axis):
    return lax.ppermute(value, axis, [(0, 1), (1, 0)])


def exchange(value, axis):
    me = lax.axis_index(axis)
    other = swap(lax.dynamic_index_in_dim(value, 1 - me, 0, keepdims=False), axis)
    mine = lax.dynamic_index_in_dim(value, me, 0, keepdims=False)
    first = jnp.where(me == 0, mine, other)
    second = jnp.where(me == 0, other, mine)
    return jnp.stack([first, second])


def pair_gather(value, axis):
    me = lax.axis_index(axis)
    other = swap(value, axis)
    return jnp.stack([jnp.where(me == 0, value, other), jnp.where(me == 0, other, value)])


def dot(left, right):
    return jnp.dot(left, right, preferred_element_type=F32)


def dot_rows(left, right):
    return lax.dot_general(left, right, (((0,), (0,)), ((), ())), preferred_element_type=F32)


def dot_cols(left, right):
    return lax.dot_general(left, right, (((1,), (1,)), ((), ())), preferred_element_type=F32)


def attention_body(q_ref, k_ref, v_ref, g_ref, c_ref, s1_ref, s2_ref, row_ref, col_ref,
                   ctx_ref, gq_ref, gk_ref, gv_ref):
    cosine, sin1, sin2 = c_ref[...], s1_ref[...], s2_ref[...]
    width = 4 * HD
    half = ROT // 2

    def turn(value):
        return (
            value * cosine
            - pltpu.roll(value, width - half, 1) * sin1
            + pltpu.roll(value, half, 1) * sin2
        )

    def turn_back(value):
        return (
            value * cosine
            + pltpu.roll(value, width - half, 1) * sin1
            - pltpu.roll(value, half, 1) * sin2
        )

    query = turn(q_ref[...]).astype(BF)
    key = turn(k_ref[...]).astype(BF)
    values = v_ref[...].astype(BF)
    grad = g_ref[...].astype(BF)
    rows = lax.broadcasted_iota(jnp.int32, (SEQ, SEQ), 0)
    cols = lax.broadcasted_iota(jnp.int32, (SEQ, SEQ), 1)
    allowed = (cols <= rows) & (col_ref[...] == row_ref[0])
    contexts, gqs, gks, gvs = [], [], [], []
    for head in range(4):
        part = slice(head * HD, (head + 1) * HD)
        qh, kh, vh, gh = query[:, part], key[:, part], values[:, part], grad[:, part]
        scores = jnp.where(allowed, SCALE * dot_cols(qh, kh), -1e30)
        top = jnp.max(scores, axis=-1, keepdims=True)
        expo = jnp.exp(scores - top)
        probs = expo * (1.0 / jnp.sum(expo, axis=-1, keepdims=True))
        probs_b = probs.astype(BF)
        contexts.append(dot(probs_b, vh))
        grad_probs = dot_cols(gh, vh)
        gvs.append(dot_rows(probs_b, gh))
        inner = jnp.sum(probs * grad_probs, axis=-1, keepdims=True)
        grad_scores = (probs * (grad_probs - inner)).astype(BF)
        gqs.append(SCALE * dot(grad_scores, kh))
        gks.append(SCALE * dot_rows(grad_scores, qh))
    ctx_ref[...] = jnp.concatenate(contexts, axis=1).astype(BF)
    gv_ref[...] = jnp.concatenate(gvs, axis=1).astype(BF)
    gq_ref[...] = turn_back(jnp.concatenate(gqs, axis=1)).astype(BF)
    gk_ref[...] = turn_back(jnp.concatenate(gks, axis=1)).astype(BF)


def attention(query, key, values, grad, cosine, sin1, sin2, segment):
    block = pl.BlockSpec((SEQ, 4 * HD), lambda i: (i, 0))
    out = jax.ShapeDtypeStruct((TOKENS, 4 * HD), BF)
    return pl.pallas_call(
        attention_body,
        grid=(TOKENS // SEQ,),
        in_specs=[block] * 7
        + [
            pl.BlockSpec((1, 1, SEQ), lambda i: (i, 0, 0)),
            pl.BlockSpec((SEQ, 1), lambda i: (i, 0)),
        ],
        out_specs=[block] * 4,
        out_shape=[out] * 4,
        compiler_params=pltpu.CompilerParams(vmem_limit_bytes=40 << 20),
        cost_estimate=pl.CostEstimate(
            flops=7 * 2 * 16 * SEQ * SEQ * HD, bytes_accessed=12 << 20, transcendentals=16 * SEQ * SEQ
        ),
        name="attention",
    )(query, key, values, grad, cosine, sin1, sin2, segment.reshape(4, 1, SEQ), segment.reshape(TOKENS, 1))


def gather_plane(value):
    return lax.all_gather(value, PLANE, axis=0, tiled=False)


def scatter_plane(value):
    return lax.psum_scatter(value, PLANE, scatter_dimension=0, tiled=False)


def gather_group(value):
    return lax.all_gather(value, GROUP, axis=0, tiled=True)


def scatter_group(value):
    return lax.psum_scatter(value, GROUP, scatter_dimension=0, tiled=True)


def owner_order(vector):
    lead = vector.shape[:-1]
    size = vector.shape[-1] // 32
    return jnp.swapaxes(vector.reshape(*lead, 2, 16, size), -3, -2).reshape(*lead, -1)


def plain_order(vector):
    lead = vector.shape[:-1]
    size = vector.shape[-1] // 32
    return jnp.swapaxes(vector.reshape(*lead, 16, 2, size), -3, -2).reshape(*lead, -1)


def local(
    hidden_in, norm_gain, norm_shift, qkv_weight, qkv_bias, proj_weight, proj_bias,
    up_weight, up_bias, down_weight, down_bias, segment_ids, positions, cotangent,
):
    xh, core, xl = lax.axis_index("xh"), lax.axis_index("core"), lax.axis_index("xl")
    hidden_own = hidden_in.reshape(128, D)
    cot_own = cotangent.reshape(128, D)

    hid = gather_group(owner_order(hidden_own))
    marks = jnp.stack(
        [positions.reshape(128), lax.dynamic_slice_in_dim(segment_ids.reshape(SEQ), xl * 128, 128)]
    )
    marks = pair_gather(pair_gather(pair_gather(marks, "xl"), "core"), "xh")
    marks = marks.transpose(3, 0, 1, 2, 4).reshape(2, TOKENS)
    position_all, segment_all = marks[0], marks[1]
    cot = gather_group(cot_own)

    qkv_parts = lax.dynamic_index_in_dim(
        qkv_weight.reshape(32, 3, 2, 2, 2, 256), xl, 4, keepdims=False
    ).transpose(2, 3, 1, 0, 4).reshape(2, 2, 96, 256)
    small = jnp.concatenate([norm_gain, norm_shift, proj_bias, down_bias, qkv_bias, up_bias])
    small = jnp.pad(small, (0, 16 * 256 - 352)).reshape(1, 1, 16, 256)
    pre2 = jnp.concatenate([qkv_parts, jnp.broadcast_to(small, (2, 2, 16, 256))], axis=2)
    pre2 = exchange(pre2, "xh")
    pre2 = exchange(pre2.swapaxes(0, 1), "core").swapaxes(0, 1)
    proj_part = lax.dynamic_slice_in_dim(proj_weight, xl * 16, 16, 0)
    proj_part = proj_part.reshape(16, 8, 256).swapaxes(0, 1).reshape(128, 256)
    pack2 = gather_plane(jnp.concatenate([pre2.reshape(448, 256), proj_part], axis=0))

    pre1 = lax.dynamic_index_in_dim(
        up_weight.reshape(32, 2, 16, 2, 2, 64), xl, 4, keepdims=False
    ).transpose(1, 3, 0, 2, 4).reshape(2, 2, 32, 1024)
    pre1 = exchange(pre1, "xh")
    pre1 = exchange(pre1.swapaxes(0, 1), "core").swapaxes(0, 1)
    down_part = lax.dynamic_slice_in_dim(down_weight, xl * 64, 64, 0)
    pack1 = gather_plane(
        jnp.concatenate([pre1.reshape(128, 1024), down_part[:, :1024], down_part[:, 1024:]], axis=0)
    )

    columns = pack2[:, :448].reshape(16, 4, 112, 256)
    q_w = columns[:, :, :32].reshape(D, 256)
    k_w = columns[:, :, 32:64].reshape(D, 256)
    v_w = columns[:, :, 64:96].reshape(D, 256)
    small = columns[:, :, 96:98].reshape(16, 2, 2, 512).astype(F32)
    gain = small[..., :32].reshape(D)
    shift = small[..., 32:64].reshape(D)
    out_bias = plain_order((small[..., 64:96] + small[..., 96:128]).reshape(D))
    qkv_b = plain_order(small[..., 128:224].reshape(3 * D)).reshape(3, 2, 2, 2, 256)
    qkv_b = qkv_b[:, xh, core, xl]
    up_b = lax.dynamic_slice_in_dim(small[:, xh, core, 224:352], xl * 64, 64, 1).reshape(1024)
    proj_rows = pack2[:, 448:].reshape(2, 2, 4, 8, 16, 256)
    proj_rows = exchange(proj_rows, "core")
    proj_rows = exchange(proj_rows.swapaxes(0, 1), "xl")
    proj_w = proj_rows.transpose(2, 1, 0, 4, 3, 5).reshape(256, D)
    up_w = pack1[:, :128].reshape(D, 1024)
    down_w = jnp.concatenate(
        [pack1[:, 128:192].reshape(1024, 1024), pack1[:, 192:].reshape(1024, 1024)], axis=1
    )

    lane = jnp.arange(128) % HD
    freqs = 10000.0 ** (-(lane % 16).astype(F32) * (2.0 / ROT))
    angles = position_all.astype(F32)[:, None] * freqs
    cosine = jnp.where(lane < ROT, jnp.cos(angles), 1.0)
    sine = jnp.sin(angles)
    sin1 = jnp.where(lane < 16, sine, 0.0)
    sin2 = jnp.where((lane >= 16) & (lane < ROT), sine, 0.0)
    cosine, sin1, sin2 = (jnp.concatenate([t, t], axis=1) for t in (cosine, sin1, sin2))

    hid_f = hid.astype(F32)
    mean = jnp.mean(hid_f, axis=-1, keepdims=True)
    centered = hid_f - mean
    rstd = lax.rsqrt(jnp.mean(centered * centered, axis=-1, keepdims=True) + EPS)
    normal = centered * rstd
    normed = (normal * gain + shift).astype(BF)
    query = dot(normed, q_w) + qkv_b[0]
    key = dot(normed, k_w) + qkv_b[1]
    values = dot(normed, v_w) + qkv_b[2]
    grad_context = dot_cols(cot, proj_w).astype(BF)
    context, grad_q, grad_k, grad_v = attention(
        query, key, values, grad_context, cosine, sin1, sin2, segment_all
    )
    upper = dot(normed, up_w) + up_b
    active, gelu_pull = jax.vjp(lambda value: jax.nn.gelu(value, approximate=True), upper)
    active = active.astype(BF)
    grad_upper = gelu_pull(dot_cols(cot, down_w))[0].astype(BF)
    branch = dot(context, proj_w) + dot(active, down_w)
    branch = scatter_group(branch.astype(BF))
    block_out = hidden_own.astype(F32) + branch.astype(F32) + out_bias
    block_out = block_out.astype(BF).reshape(1, 128, D)

    grad_normed = (
        dot_cols(grad_q, q_w) + dot_cols(grad_k, k_w) + dot_cols(grad_v, v_w) + dot_cols(grad_upper, up_w)
    )
    gain_sum = jnp.sum(grad_normed * normal, axis=0)
    shift_sum = jnp.sum(grad_normed, axis=0)
    out_sum = owner_order(jnp.sum(cot_own.astype(F32), axis=0))
    grad_own = scatter_group(grad_normed.astype(BF)).astype(F32)

    own = owner_order(hidden_own).astype(F32)
    mean = jnp.mean(own, axis=-1, keepdims=True)
    centered = own - mean
    rstd = lax.rsqrt(jnp.mean(centered * centered, axis=-1, keepdims=True) + EPS)
    normal_own = centered * rstd
    scaled = grad_own * gain
    inner = jnp.mean(scaled * normal_own, axis=-1, keepdims=True)
    pulled = (scaled - jnp.mean(scaled, axis=-1, keepdims=True) - normal_own * inner) * rstd
    grad_hidden = (cot_own.astype(F32) + plain_order(pulled)).reshape(1, 128, D)

    grad_proj = dot_rows(context, cot).astype(BF)
    grad_down = dot_rows(active, cot).astype(BF)
    grad_up = dot_rows(normed, grad_upper).astype(BF)
    grad_qw, grad_kw, grad_vw = (
        dot_rows(normed, g).astype(BF).reshape(16, 4, 32, 256) for g in (grad_q, grad_k, grad_v)
    )
    bias_sums = [jnp.sum(g.astype(F32), axis=0) for g in (grad_q, grad_k, grad_v)]
    qkv_sum = jnp.zeros((3, 2, 2, 2, 256), F32)
    qkv_sum = lax.dynamic_update_slice(
        qkv_sum, jnp.stack(bias_sums).reshape(3, 1, 1, 1, 256), (0, xh, core, xl, 0)
    )
    qkv_sum = owner_order(qkv_sum.reshape(3 * D)).reshape(16, 4, 96)
    up_sum = jnp.zeros((16, 2, 2, 2, 64), F32)
    up_sum = lax.dynamic_update_slice(
        up_sum, jnp.sum(grad_upper.astype(F32), axis=0).reshape(16, 1, 1, 1, 64), (0, xh, core, xl, 0)
    ).reshape(16, 4, 128)
    sums = jnp.concatenate(
        [s.reshape(16, 4, 32) for s in (gain_sum, shift_sum, out_sum)] + [qkv_sum, up_sum], axis=2
    )
    sums = jnp.pad(sums, ((0, 0), (0, 0), (0, 16 * 256 - 320))).reshape(16, 4, 16, 256).astype(BF)
    cols2 = jnp.concatenate([grad_qw, grad_kw, grad_vw, sums], axis=2).reshape(16, 448, 256)
    grad_proj = grad_proj.reshape(4, 2, 2, 16, 8, 256).transpose(1, 2, 0, 4, 3, 5)
    grad_proj = exchange(grad_proj, "core")
    grad_proj = exchange(grad_proj.swapaxes(0, 1), "xl").swapaxes(0, 1).reshape(16, 128, 256)
    back2 = scatter_plane(jnp.concatenate([cols2, grad_proj], axis=1))
    back1 = scatter_plane(
        jnp.concatenate(
            [
                grad_up.reshape(16, 128, 1024),
                grad_down[:, :1024].reshape(16, 64, 1024),
                grad_down[:, 1024:].reshape(16, 64, 1024),
            ],
            axis=1,
        )
    )

    def to_owner(value):
        value = exchange(value.swapaxes(0, 1), "core")
        value = exchange(value.swapaxes(0, 1), "xh")
        return pair_gather(value, "xl")

    own1 = to_owner(back1[:128].reshape(2, 2, 32, 1024))
    grad_up = own1.reshape(2, 2, 2, 32, 16, 64).transpose(3, 1, 4, 2, 0, 5).reshape(32, FF)
    own2 = to_owner(back2[:448].reshape(2, 2, 112, 256))
    grad_qkv = own2[:, :, :, :96].reshape(2, 2, 2, 3, 32, 256).transpose(4, 3, 1, 2, 0, 5)
    grad_qkv = grad_qkv.reshape(32, 3 * D)
    sums = jnp.sum(own2[:, :, :, 96:98].astype(F32), axis=(0, 1, 2)).reshape(512)
    grad_down = pair_gather(
        jnp.concatenate([back1[128:192], back1[192:]], axis=1), "xl"
    ).reshape(128, D)
    grad_proj = pair_gather(
        back2[448:].reshape(8, 16, 256).swapaxes(0, 1).reshape(16, D), "xl"
    ).reshape(32, D)
    return (
        block_out,
        grad_hidden,
        sums[:32],
        sums[32:64],
        grad_qkv.astype(F32),
        sums[96:192],
        grad_proj.astype(F32),
        sums[64:96],
        grad_up.astype(F32),
        sums[192:320],
        grad_down.astype(F32),
        sums[64:96],
    )


def solution(mesh):
    cut = Mesh(mesh.devices.reshape(2, 4, 4, 2, 2), AXES)
    row, vec = P(SHARD, None), P(SHARD)
    tok = P(SHARD, "xl", None)
    return jax.shard_map(
        local,
        mesh=cut,
        in_specs=(
            tok, vec, vec, row, vec, row, vec, row, vec, row, vec, row, P(SHARD, "xl"), tok,
        ),
        out_specs=(tok, tok, vec, vec, row, vec, row, vec, row, vec, row, vec),
        check_vma=False,
    )
```

```python
import math

import jax
import jax.numpy as jnp
from jax import lax
from jax.experimental import pallas as pl
from jax.experimental.pallas import tpu as pltpu
from jax.sharding import Mesh, PartitionSpec as P

D = 2048
H = 32
HD = 64
ROT = 32
FF = 8192
SEQ = 256
SCALE = HD**-0.5
EPS = 1e-5
VMEM = 60 << 20
AXES = ("xh", "z", "y", "core", "xl")
SHARD = ("xh", "z", "y", "core")
PLANE = ("z", "y")
TOKENS = 1024
BF = jnp.bfloat16
F32 = jnp.float32


def shift(value, axis, step):
    names, size = (("xh", "xl"), 4) if axis == "x" else (axis, lax.axis_size(axis))
    return lax.ppermute(value, names, [(i, (i + step) % size) for i in range(size)])


def pick(value, index, axis=0):
    return lax.dynamic_index_in_dim(value, index, axis, keepdims=False)


def tie(*values):
    return lax.optimization_barrier(values)


def ring_first(value):
    return shift(value, "x", 1), shift(value, "x", -1)


def ring_second(below, above):
    return shift(below[:64], "x", 1), shift(above[64:], "x", -1)


def fold_first(parts):
    far = parts[2].astype(BF)
    return shift(far[:64], "x", 1), shift(far[64:], "x", -1)


def fold_second(parts, low, high):
    after_me = jnp.concatenate([parts[1][:64] + low.astype(F32), parts[1][64:]]).astype(BF)
    before_me = jnp.concatenate([parts[3][:64], parts[3][64:] + high.astype(F32)]).astype(BF)
    return shift(after_me, "x", 1), shift(before_me, "x", -1)


def sum_parts(near, other):
    near, other = near.reshape(4, 128, D), other.reshape(4, 128, D)
    return [near[k].astype(F32) + other[k].astype(F32) for k in range(4)]


def exchange4(parts):
    xh, core = lax.axis_index("xh"), lax.axis_index("core")
    rel = [parts[0]]
    for turn in (1, 2, 3):
        rel.append(lax.ppermute(parts[turn], ("xh", "core"), [(i, i ^ turn) for i in range(4)]))
    me = 2 * xh + core
    rel = jnp.stack(rel)
    return jnp.concatenate([pick(rel, me ^ source) for source in range(4)])


def pair_gather(value, axis):
    me = lax.axis_index(axis)
    rel = jnp.stack([value, shift(value, axis, 1)])
    return jnp.where(me == 0, rel, rel[::-1])


def gather_plane(value):
    return lax.all_gather(value, PLANE, axis=0, tiled=False)


def scatter_plane_whole(value):
    flat = value.reshape(-1, value.shape[-1])
    return lax.psum_scatter(flat, PLANE, scatter_dimension=0, tiled=True)


STEPS = (("core", 1), ("y", 1), ("y", 2), ("z", 1), ("z", 2), ("xh", 1))


def toward(value, axis, bit):
    size = lax.axis_size(axis)
    return lax.ppermute(value, axis, [(i, i ^ bit) for i in range(size)])


def gather_step(value, step):
    axis, bit = STEPS[step]
    other = toward(value, axis, bit)
    high = (lax.axis_index(axis) & bit) != 0
    return jnp.concatenate([jnp.where(high, other, value), jnp.where(high, value, other)])


def reduce_step(value, step):
    axis, bit = STEPS[step]
    parts = value.reshape(2, value.shape[0] // 2, value.shape[1])
    mine = jnp.where((lax.axis_index(axis) & bit) != 0, 1, 0)
    return pick(parts, mine) + toward(pick(parts, 1 - mine), axis, bit)


def rehome(value, back=False):
    pairs = []
    for z in range(4):
        for y in range(4):
            for core in range(2):
                for xl in range(2):
                    owner = ((z * 4 + y) * 2 + core) * 2 + xl
                    user = ((y * 4 + 2 * core + xl) * 2 + z // 2) * 2 + z % 2
                    pairs.append((user, owner) if back else (owner, user))
    return lax.ppermute(value, ("z", "y", "core", "xl"), pairs)


def after(value, *others):
    return lax.optimization_barrier((value, *others))[0]


def owner_order(vector):
    lead = vector.shape[:-1]
    size = vector.shape[-1] // 32
    return jnp.swapaxes(vector.reshape(*lead, 2, 16, size), -3, -2).reshape(*lead, -1)


def plain_order(vector):
    lead = vector.shape[:-1]
    size = vector.shape[-1] // 32
    return jnp.swapaxes(vector.reshape(*lead, 16, 2, size), -3, -2).reshape(*lead, -1)


def dot(left, right):
    return jnp.dot(left, right, preferred_element_type=F32)


def dot_rows(left, right):
    return lax.dot_general(left, right, (((0,), (0,)), ((), ())), preferred_element_type=F32)


def dot_cols(left, right):
    return lax.dot_general(left, right, (((1,), (1,)), ((), ())), preferred_element_type=F32)


def deal_body(place_ref, up_ref, qkv_ref, out_ref):
    me, xl = place_ref[0], place_ref[1]
    lane = lax.broadcasted_iota(jnp.int32, (32, 128), 1)
    for turn in range(4):
        target = me ^ turn
        xh, core = lax.div(target, 2), lax.rem(target, 2)
        for pair in range(8):
            start = xh * 4096 + core * 128 + pair * 512
            left = up_ref[:, pl.ds(pl.multiple_of(start, 128), 128)].astype(F32)
            right = up_ref[:, pl.ds(pl.multiple_of(start + 256, 128), 128)].astype(F32)
            left = jnp.where(xl == 0, left, pltpu.roll(left, 64, 1))
            right = jnp.where(xl == 0, pltpu.roll(right, 64, 1), right)
            both = jnp.where(lane < 64, left, right).astype(BF)
            out_ref[turn, :, pair * 128 : (pair + 1) * 128] = both
        for block in range(3):
            start = block * D + xh * 1024 + core * 512 + xl * 256
            out_ref[turn, :, 1024 + block * 256 : 1280 + block * 256] = qkv_ref[
                :, pl.ds(pl.multiple_of(start, 256), 256)
            ]


def deal(me, xl, up, qkv):
    vmem = pl.BlockSpec(memory_space=pltpu.VMEM)
    return pl.pallas_call(
        deal_body,
        in_specs=[pl.BlockSpec(memory_space=pltpu.SMEM), vmem, vmem],
        out_specs=vmem,
        out_shape=jax.ShapeDtypeStruct((4, 32, 1792), BF),
        name="deal",
    )(jnp.stack([me, xl]).astype(jnp.int32), up, qkv)


def spread_body(place_ref, *refs):
    pieces, up_ref, qkv_ref, held = refs[:4], refs[4], refs[5], refs[6]
    place, core = place_ref[0], place_ref[1]
    for step in range(4):
        source = lax.rem(place - step + 4, 4)
        for side in range(2):
            held[source, core ^ side] = pieces[step][side]
    for xh in range(2):
        for unit in range(16):
            for core in range(2):
                block = [
                    held[2 * xh + xl, core, :32, unit * 64 : (unit + 1) * 64].astype(F32) for xl in range(2)
                ]
                start = xh * 4096 + unit * 256 + core * 128
                up_ref[:, start : start + 128] = jnp.concatenate(block, axis=1)
        for core in range(2):
            for xl in range(2):
                for block in range(3):
                    start = block * D + xh * 1024 + core * 512 + xl * 256
                    qkv_ref[:, start : start + 256] = held[
                        2 * xh + xl, core, 32:, block * 256 : (block + 1) * 256
                    ].astype(F32)


def spread(place, core, pieces):
    vmem = pl.BlockSpec(memory_space=pltpu.VMEM)
    return pl.pallas_call(
        spread_body,
        in_specs=[pl.BlockSpec(memory_space=pltpu.SMEM)] + [vmem] * 4,
        out_specs=[vmem] * 2,
        out_shape=[jax.ShapeDtypeStruct((32, FF), F32), jax.ShapeDtypeStruct((32, 3 * D), F32)],
        scratch_shapes=[pltpu.VMEM((4, 2, 64, 1024), BF)],
        name="spread",
    )(jnp.stack([place, core]).astype(jnp.int32), *pieces)


def sort_body(core_ref, in_ref, near_ref, far_ref, down_ref, proj_ref):
    core = core_ref[0]
    for xh in range(2):
        for ref, which in ((near_ref, core), (far_ref, 1 - core)):
            start = pl.multiple_of(xh * 64 + which * 32, 32)
            ref[xh, :32] = in_ref[pl.ds(start, 32), :]
            ref[xh, 32:] = in_ref[pl.ds(pl.multiple_of(start + 256, 32), 32), :]
    down_ref[:, :1024] = in_ref[128:192, :]
    down_ref[:, 1024:] = in_ref[192:256, :]
    for block in range(8):
        proj_ref[:, block * 256 : (block + 1) * 256] = in_ref[
            256 + block * 16 : 272 + block * 16, 768:
        ]


def sort(core, summed):
    vmem = pl.BlockSpec(memory_space=pltpu.VMEM)
    return pl.pallas_call(
        sort_body,
        in_specs=[pl.BlockSpec(memory_space=pltpu.SMEM), vmem],
        out_specs=[vmem] * 4,
        out_shape=[
            jax.ShapeDtypeStruct((2, 64, 1024), BF),
            jax.ShapeDtypeStruct((2, 64, 1024), BF),
            jax.ShapeDtypeStruct((64, D), BF),
            jax.ShapeDtypeStruct((16, D), BF),
        ],
        name="sort",
    )(core.reshape(1).astype(jnp.int32), summed)


def norm_body(near_ref, far_ref, gain_ref, shift_ref, normed_ref, turned_ref, mean_ref, rstd_ref):
    hidden = jnp.where(pl.program_id(0) < 2, near_ref[...], far_ref[...]).astype(F32)
    mean = jnp.mean(hidden, axis=-1, keepdims=True)
    centered = hidden - mean
    rstd = lax.rsqrt(jnp.mean(centered * centered, axis=-1, keepdims=True) + EPS)
    normed = (centered * rstd * gain_ref[...] + shift_ref[...]).astype(BF)
    normed_ref[...] = normed
    turned_ref[...] = normed.T
    mean_ref[...] = mean
    rstd_ref[...] = rstd


def norm(near, far, gain, shift_row):
    step = 256
    row = pl.BlockSpec((step, D), lambda i: (i, 0))
    vec = pl.BlockSpec((1, D), lambda i: (0, 0))
    one = pl.BlockSpec((step, 1), lambda i: (i, 0))
    return pl.pallas_call(
        norm_body,
        grid=(TOKENS // step,),
        in_specs=[
            pl.BlockSpec((step, D), lambda i: (jnp.minimum(i, 1), 0)),
            pl.BlockSpec((step, D), lambda i: (jnp.maximum(i - 2, 0), 0)),
            vec,
            vec,
        ],
        out_specs=[row, pl.BlockSpec((D, step), lambda i: (0, i)), one, one],
        out_shape=[
            jax.ShapeDtypeStruct((TOKENS, D), BF),
            jax.ShapeDtypeStruct((D, TOKENS), BF),
            jax.ShapeDtypeStruct((TOKENS, 1), F32),
            jax.ShapeDtypeStruct((TOKENS, 1), F32),
        ],
        compiler_params=pltpu.CompilerParams(vmem_limit_bytes=VMEM),
        cost_estimate=pl.CostEstimate(flops=20 << 20, bytes_accessed=12 << 20, transcendentals=0),
        name="norm",
    )(near, far, gain.reshape(1, D), shift_row.reshape(1, D))


def heads_body(odd_ref, normed_hbm, turned_hbm, near_hbm, far_hbm, weights_hbm, bias_ref, cos_hbm,
               sin1_hbm, sin2_hbm, row_ref, col_hbm, ctx_hbm, out_hbm, pack_hbm,
               cos_ref, sin1_ref, sin2_ref, col_ref, normed, turned, cot, ctx_ref, out_ref, weights, proj, merged, queries, keys, values, grads, mask, raw, pulled,
               probs, slopes, back_q, back_k, packed, sem, out_sems):
    width = 4 * HD
    half = ROT // 2
    loads = [
        pltpu.make_async_copy(weights_hbm.at[:, pl.ds(256, 128), :], weights, sem.at[0]),
        pltpu.make_async_copy(normed_hbm, normed, sem.at[1]),
        pltpu.make_async_copy(near_hbm, cot.at[pl.ds(0, 512)], sem.at[2]),
        pltpu.make_async_copy(far_hbm, cot.at[pl.ds(512, 512)], sem.at[3]),
        pltpu.make_async_copy(turned_hbm, turned, sem.at[4]),
        pltpu.make_async_copy(cos_hbm, cos_ref, sem.at[5]),
        pltpu.make_async_copy(sin1_hbm, sin1_ref, sem.at[6]),
        pltpu.make_async_copy(sin2_hbm, sin2_ref, sem.at[7]),
        pltpu.make_async_copy(col_hbm, col_ref, sem.at[8]),
    ]
    for place in (0, 1, 5, 6, 7, 8, 2, 3, 4):
        loads[place].start()
    odd = odd_ref[0]
    for k in range(2):
        probs[k, :128, 128:] = jnp.zeros((128, 128), BF)
        slopes[k, :128, 128:] = jnp.zeros((128, 128), BF)

    def sides(item):
        pair, base = lax.rem(item, 2), lax.div(item, 2) * 512
        first = pl.multiple_of(base + lax.rem(2 * pair + 3 * odd, 4) * 128, 128)
        second = pl.multiple_of(base + lax.rem(2 * pair + 3 * odd + 1, 4) * 128, 128)
        return first, second

    for place in (0, 1, 5, 6, 7, 8):
        loads[place].wait()
    for block in range(8):
        proj[:, block * 256 : (block + 1) * 256] = weights[
            :, block * 16 : (block + 1) * 16, 768:
        ].reshape(256, 256)

    @pl.loop(0, 4)
    def _(step):
        rows = pl.ds(pl.multiple_of(step * 256, 256), 256)
        merged[...] = dot(normed[rows, :], weights[:, :, :768].reshape(D, 768)) + bias_ref[...]
        @pl.loop(0, 8)
        def _(part):
            here = pl.ds(pl.multiple_of(part * 32, 32), 32)
            there = pl.ds(pl.multiple_of(step * 256 + part * 32, 32), 32)
            cosine, sin1, sin2 = cos_ref[there, :], sin1_ref[there, :], sin2_ref[there, :]
            for pair in range(2):
                for ref, base in ((queries, 0), (keys, width)):
                    value = merged[here, base + pair * 128 : base + (pair + 1) * 128]
                    value = (
                        value * cosine
                        - pltpu.roll(value, 128 - half, 1) * sin1
                        + pltpu.roll(value, half, 1) * sin2
                    )
                    ref[pair, there, :] = (value * SCALE if base == 0 else value).astype(BF)
                start = 2 * width + pair * 128
                values[pair, there, :] = merged[here, start : start + 128].astype(BF)

    loads[2].wait()
    loads[3].wait()

    @pl.loop(0, 2)
    def _(step):
        rows = pl.ds(pl.multiple_of(step * 512, 512), 512)
        pulls = dot_cols(cot[rows, :], proj[...]).astype(BF)
        for pair in range(2):
            grads[pair, rows, :] = pulls[:, pair * 128 : (pair + 1) * 128]

    lane = lax.broadcasted_iota(jnp.int32, (SEQ, 128), 1)
    low = lane < HD

    @pl.loop(0, 4)
    def _(item):
        first, second = sides(item)
        segment = row_ref[item]
        for start in range(0, SEQ, 64):
            side = first if start < 128 else second
            rows = lax.broadcasted_iota(jnp.int32, (64, SEQ), 0) + start
            cols = lax.broadcasted_iota(jnp.int32, (64, SEQ), 1)
            own = col_ref[pl.ds(pl.multiple_of(side + start % 128, 64), 64), :]
            allowed = (cols <= rows) & (own == segment)
            mask[start : start + 64, :] = jnp.where(allowed, 0.0, -1e30)

        for pair in range(2):

            def load(ref):
                return jnp.concatenate([ref[pair, pl.ds(first, 128), :], ref[pair, pl.ds(second, 128), :]])

            query, key, value, grad = load(queries), load(keys), load(values), load(grads)
            for k in range(2):
                own = low if k == 0 else ~low
                raw[k] = dot_cols(jnp.where(own, query, 0), key)
                pulled[k] = dot_cols(jnp.where(own, grad, 0), value)
            for k in range(2):
                for start in range(0, SEQ, 32):
                    size = 128 if start < 128 else SEQ
                    rows = slice(start, start + 32)
                    scores = raw[k, rows, :size] + mask[rows, :size]
                    top = jnp.max(scores, axis=-1, keepdims=True)
                    expo = jnp.exp(scores - top)
                    prob = expo * (1.0 / jnp.sum(expo, axis=-1, keepdims=True))
                    probs[k, rows, :size] = prob.astype(BF)
                    grad_prob = pulled[k, rows, :size]
                    inner = jnp.sum(prob * grad_prob, axis=-1, keepdims=True)
                    slopes[k, rows, :size] = (prob * (grad_prob - inner)).astype(BF)
            context = jnp.where(low, dot(probs[0], value), dot(probs[1], value)).astype(BF)
            grad_v = jnp.where(low, dot_rows(probs[0], grad), dot_rows(probs[1], grad)).astype(BF)
            back_q[...] = SCALE * jnp.where(low, dot(slopes[0], key), dot(slopes[1], key))
            back_k[...] = jnp.where(low, dot_rows(slopes[0], query), dot_rows(slopes[1], query))
            lanes = slice(pair * 128, (pair + 1) * 128)
            for at, side in ((0, first), (128, second)):
                rows = pl.ds(side, 128)
                ctx_ref[rows, lanes] = context[at : at + 128]
                out_ref[rows, 2 * width + pair * 128 : 2 * width + (pair + 1) * 128] = grad_v[at : at + 128]
                for start in range(0, 128, 32):
                    there = pl.ds(pl.multiple_of(side + start, 32), 32)
                    cosine, sin1, sin2 = cos_ref[there, :], sin1_ref[there, :], sin2_ref[there, :]
                    for ref, base in ((back_q, 0), (back_k, width)):
                        turned_back = ref[at + start : at + start + 32, :]
                        turned_back = (
                            turned_back * cosine
                            + pltpu.roll(turned_back, 128 - half, 1) * sin1
                            - pltpu.roll(turned_back, half, 1) * sin2
                        )
                        out_ref[there, base + pair * 128 : base + (pair + 1) * 128] = turned_back.astype(BF)

    def store(step):
        owners = pl.ds(step * 2, 2)
        return pltpu.make_async_copy(
            packed.at[owners], pack_hbm.at[owners, pl.ds(256, 128), :], out_sems.at[step]
        )

    ctx_store = pltpu.make_async_copy(ctx_ref, ctx_hbm, sem.at[0])
    out_store = pltpu.make_async_copy(out_ref, out_hbm, sem.at[1])
    ctx_store.start()
    out_store.start()

    total = dot_rows(ctx_ref[...], cot[...]).astype(BF)
    for block in range(8):
        packed[:, block * 16 : (block + 1) * 16, 768:] = total[
            :, block * 256 : (block + 1) * 256
        ].reshape(16, 16, 256)
    loads[4].wait()

    @pl.loop(0, 8)
    def _(step):
        rows = pl.ds(pl.multiple_of(step * 256, 256), 256)
        total = dot(turned[rows, :], out_ref[...]).astype(BF)
        packed[pl.ds(step * 2, 2), :, :768] = total.reshape(2, 128, 768)
        store(step).start()

    ctx_store.wait()
    out_store.wait()

    @pl.loop(0, 8)
    def _(step):
        store(step).wait()


def heads(odd, normed, turned, near, far, weights, bias, cosine, sin1, sin2, segment):
    blocks = segment.reshape(2, 4, 128)
    rows = jnp.where(odd == 0, blocks, jnp.roll(blocks, 1, axis=1)).reshape(4, 1, SEQ)
    vmem, hbm = pl.BlockSpec(memory_space=pltpu.VMEM), pl.BlockSpec(memory_space=pltpu.HBM)
    table = pltpu.VMEM((TOKENS, 128), F32)
    head_b = pltpu.VMEM((2, TOKENS, 128), BF)
    head_f = pltpu.VMEM((SEQ, 128), F32)
    return pl.pallas_call(
        heads_body,
        in_specs=[pl.BlockSpec(memory_space=pltpu.SMEM)] + [hbm] * 5 + [vmem] + [hbm] * 3 + [vmem, hbm],
        out_specs=[hbm] * 3,
        out_shape=[
            jax.ShapeDtypeStruct((TOKENS, 4 * HD), BF),
            jax.ShapeDtypeStruct((TOKENS, 12 * HD), BF),
            jax.ShapeDtypeStruct((16, 384, 1024), BF),
        ],
        scratch_shapes=[
            table,
            table,
            table,
            pltpu.VMEM((TOKENS, 1), jnp.int32),
            pltpu.VMEM((TOKENS, D), BF),
            pltpu.VMEM((D, TOKENS), BF),
            pltpu.VMEM((TOKENS, D), BF),
            pltpu.VMEM((TOKENS, 4 * HD), BF),
            pltpu.VMEM((TOKENS, 12 * HD), BF),
            pltpu.VMEM((16, 128, 1024), BF),
            pltpu.VMEM((256, D), BF),
            pltpu.VMEM((256, 12 * HD), F32),
            head_b,
            head_b,
            head_b,
            head_b,
            pltpu.VMEM((SEQ, SEQ), F32),
            pltpu.VMEM((2, SEQ, SEQ), F32),
            pltpu.VMEM((2, SEQ, SEQ), F32),
            pltpu.VMEM((2, SEQ, SEQ), BF),
            pltpu.VMEM((2, SEQ, SEQ), BF),
            head_f,
            head_f,
            pltpu.VMEM((16, 128, 1024), BF),
            pltpu.SemaphoreType.DMA((9,)),
            pltpu.SemaphoreType.DMA((8,)),
        ],
        compiler_params=pltpu.CompilerParams(vmem_limit_bytes=VMEM),
        cost_estimate=pl.CostEstimate(
            flops=14 << 30, bytes_accessed=40 << 20, transcendentals=16 * SEQ * SEQ
        ),
        name="heads",
    )(
        odd.reshape(1), normed, turned, near, far, weights, bias, cosine, sin1, sin2, rows,
        segment.reshape(TOKENS, 1),
    )


def feed_body(normed_hbm, turned_hbm, near_hbm, far_hbm, weights_hbm, bias_ref, pack_in,
              act_hbm, grad_hbm, pack_hbm,
              normed, turned, cot, up, down, act, grads, upper_ref, slope_ref, up_out, down_out,
              sems, act_sems, grad_sems, up_sems, down_sems):
    up_load = pltpu.make_async_copy(weights_hbm.at[:, pl.ds(0, 128), :], up, sems.at[0])
    down_load = pltpu.make_async_copy(weights_hbm.at[:, pl.ds(128, 128), :], down, sems.at[1])
    normed_load = pltpu.make_async_copy(normed_hbm, normed, sems.at[2])
    near_load = pltpu.make_async_copy(near_hbm, cot.at[pl.ds(0, 512)], sems.at[3])
    far_load = pltpu.make_async_copy(far_hbm, cot.at[pl.ds(512, 512)], sems.at[4])
    turned_load = pltpu.make_async_copy(turned_hbm, turned, sems.at[5])
    for load in (up_load, normed_load, down_load, near_load, far_load, turned_load):
        load.start()

    def act_store(step):
        rows = pl.ds(pl.multiple_of(step * 256, 256), 256)
        return pltpu.make_async_copy(act.at[rows, :], act_hbm.at[rows, :], act_sems.at[step])

    def grad_store(step):
        rows = pl.ds(pl.multiple_of(step * 256, 256), 256)
        return pltpu.make_async_copy(grads.at[rows, :], grad_hbm.at[rows, :], grad_sems.at[step])

    def up_store(step):
        owners = pl.ds(step * 2, 2)
        return pltpu.make_async_copy(
            up_out.at[owners], pack_hbm.at[owners, pl.ds(0, 128), :], up_sems.at[step]
        )

    def down_store(step):
        owners = pl.ds(step * 4, 4)
        return pltpu.make_async_copy(
            down_out.at[owners], pack_hbm.at[owners, pl.ds(128, 128), :], down_sems.at[step]
        )

    root = math.sqrt(2.0 / math.pi)
    up_load.wait()
    normed_load.wait()

    @pl.loop(0, 4)
    def _(step):
        rows = pl.ds(pl.multiple_of(step * 256, 256), 256)
        upper_ref[rows, :] = dot(normed[rows, :], up[...].reshape(D, 1024)) + bias_ref[...]

    down_load.wait()
    near_load.wait()
    far_load.wait()

    @pl.loop(0, 4)
    def _(step):
        rows = pl.ds(pl.multiple_of(step * 256, 256), 256)
        slope_ref[...] = dot_cols(cot[rows, :1024], down[:, :64].reshape(1024, 1024)) + dot_cols(
            cot[rows, 1024:], down[:, 64:].reshape(1024, 1024)
        )

        @pl.loop(0, 16)
        def _(part):
            here = pl.ds(pl.multiple_of(part * 16, 16), 16)
            there = pl.ds(pl.multiple_of(step * 256 + part * 16, 16), 16)
            for side in range(2):
                lanes = slice(side * 512, side * 512 + 512)
                upper = upper_ref[there, lanes]
                square = upper * upper
                bend = jnp.tanh(upper * (root + (root * 0.044715) * square))
                half = 0.5 + 0.5 * bend
                slope = half + upper * (0.5 - 0.5 * (bend * bend)) * (root + (root * 3 * 0.044715) * square)
                act[there, lanes] = (upper * half).astype(BF)
                grads[there, lanes] = (slope_ref[here, lanes] * slope).astype(BF)

        act_store(step).start()
        grad_store(step).start()

    turned_load.wait()

    @pl.loop(0, 8)
    def _(step):
        rows = pl.ds(pl.multiple_of(step * 256, 256), 256)
        total = dot(turned[rows, :], grads[...]).astype(BF)
        up_out[pl.ds(step * 2, 2)] = total.reshape(2, 128, 1024)
        up_store(step).start()

    @pl.loop(0, 4)
    def _(step):
        lanes = pl.ds(pl.multiple_of(step * 256, 256), 256)
        total = dot_rows(act[:, lanes], cot[...]).astype(BF)
        down_out[pl.ds(step * 4, 4), :64] = total[:, :1024].reshape(4, 64, 1024)
        down_out[pl.ds(step * 4, 4), 64:] = total[:, 1024:].reshape(4, 64, 1024)
        down_store(step).start()

    @pl.loop(0, 4)
    def _(step):
        act_store(step).wait()
        grad_store(step).wait()
        down_store(step).wait()

    @pl.loop(0, 8)
    def _(step):
        up_store(step).wait()


def feed(normed, turned, near, far, weights, bias, pack):
    vmem, hbm = pl.BlockSpec(memory_space=pltpu.VMEM), pl.BlockSpec(memory_space=pltpu.HBM)
    return pl.pallas_call(
        feed_body,
        in_specs=[hbm] * 5 + [vmem, hbm],
        out_specs=[hbm] * 3,
        out_shape=[
            jax.ShapeDtypeStruct((TOKENS, 1024), BF),
            jax.ShapeDtypeStruct((TOKENS, 1024), BF),
            jax.ShapeDtypeStruct((16, 384, 1024), BF),
        ],
        input_output_aliases={6: 2},
        scratch_shapes=[
            pltpu.VMEM((TOKENS, D), BF),
            pltpu.VMEM((D, TOKENS), BF),
            pltpu.VMEM((TOKENS, D), BF),
            pltpu.VMEM((16, 128, 1024), BF),
            pltpu.VMEM((16, 128, 1024), BF),
            pltpu.VMEM((TOKENS, 1024), BF),
            pltpu.VMEM((TOKENS, 1024), BF),
            pltpu.VMEM((TOKENS, 1024), F32),
            pltpu.VMEM((256, 1024), F32),
            pltpu.VMEM((16, 128, 1024), BF),
            pltpu.VMEM((16, 128, 1024), BF),
            pltpu.SemaphoreType.DMA((6,)),
            pltpu.SemaphoreType.DMA((4,)),
            pltpu.SemaphoreType.DMA((4,)),
            pltpu.SemaphoreType.DMA((8,)),
            pltpu.SemaphoreType.DMA((4,)),
        ],
        compiler_params=pltpu.CompilerParams(vmem_limit_bytes=VMEM),
        cost_estimate=pl.CostEstimate(
            flops=8 * TOKENS * D * 1024, bytes_accessed=32 << 20, transcendentals=TOKENS * 1024
        ),
        name="feed",
    )(normed, turned, near, far, weights, bias, pack)


def branch_body(context_ref, proj_ref, act_ref, down_ref, near_ref, far_ref):
    total = dot(act_ref[...], down_ref[...].reshape(1024, 256))
    total = (total + dot(context_ref[...], proj_ref[...].reshape(256, 256))).astype(BF)
    near_ref[...] = total[:512]
    far_ref[...] = total[512:]


def branch_out(context, active, weights):
    return pl.pallas_call(
        branch_body,
        grid=(8,),
        in_specs=[
            pl.BlockSpec((TOKENS, 256), lambda n: (0, 0), pipeline_mode=pl.Buffered(1)),
            pl.BlockSpec((16, 16, 256), lambda n: (0, 16 + n, 3)),
            pl.BlockSpec((TOKENS, 1024), lambda n: (0, 0), pipeline_mode=pl.Buffered(1)),
            pl.BlockSpec((16, 64, 256), lambda n: (0, 2 + n // 4, n % 4)),
        ],
        out_specs=[pl.BlockSpec((512, 256), lambda n: (0, n))] * 2,
        out_shape=[jax.ShapeDtypeStruct((512, D), BF)] * 2,
        compiler_params=pltpu.CompilerParams(vmem_limit_bytes=VMEM),
        cost_estimate=pl.CostEstimate(
            flops=2 * TOKENS * D * 1280, bytes_accessed=12 << 20, transcendentals=0
        ),
        name="branch",
    )(context, weights, active, weights)


def pull_body(grad_ref, merged_ref, up_ref, qkv_ref, hid_near_ref, hid_far_ref, mean_ref, rstd_ref,
              near_ref, far_ref, gain_ref, shift_ref, up_ref_sum, qkv_ref_sum):
    total = dot_cols(grad_ref[...], up_ref[...].reshape(256, 1024))
    total = total + dot_cols(merged_ref[...], qkv_ref[...].reshape(256, 1024)[:, :768])
    near_ref[...] = total[:512].astype(BF)
    far_ref[...] = total[512:].astype(BF)
    hidden = jnp.concatenate([hid_near_ref[...], hid_far_ref[...]]).astype(F32)
    normal = (hidden - mean_ref[...]) * rstd_ref[...]
    gain_ref[...] = jnp.sum(total * normal, axis=0, keepdims=True)
    shift_ref[...] = jnp.sum(total, axis=0, keepdims=True)

    @pl.when(pl.program_id(0) == 0)
    def _():
        ones = jnp.ones((16, TOKENS), BF)
        up_ref_sum[...] = dot(ones, grad_ref[...])[:1]
        qkv_ref_sum[...] = dot(ones, merged_ref[...])[:1]


def pull(grad_upper, grad_merged, weights, near, far, mean, rstd):
    def whole(width):
        return pl.BlockSpec((TOKENS, width), lambda n: (0, 0), pipeline_mode=pl.Buffered(1))

    half = pl.BlockSpec((512, 256), lambda n: (0, n))
    vec = pl.BlockSpec((1, 256), lambda n: (0, n))
    return pl.pallas_call(
        pull_body,
        grid=(8,),
        in_specs=[
            whole(1024),
            whole(768),
            pl.BlockSpec((2, 128, 1024), lambda n: (n, 0, 0)),
            pl.BlockSpec((2, 128, 1024), lambda n: (n, 2, 0)),
            half,
            half,
            whole(1),
            whole(1),
        ],
        out_specs=[half] * 2
        + [vec, vec, pl.BlockSpec((1, 1024), lambda n: (0, 0)), pl.BlockSpec((1, 768), lambda n: (0, 0))],
        out_shape=[
            jax.ShapeDtypeStruct((512, D), BF),
            jax.ShapeDtypeStruct((512, D), BF),
            jax.ShapeDtypeStruct((1, D), F32),
            jax.ShapeDtypeStruct((1, D), F32),
            jax.ShapeDtypeStruct((1, 1024), F32),
            jax.ShapeDtypeStruct((1, 768), F32),
        ],
        compiler_params=pltpu.CompilerParams(vmem_limit_bytes=VMEM),
        cost_estimate=pl.CostEstimate(
            flops=2 * TOKENS * D * 1792, bytes_accessed=16 << 20, transcendentals=0
        ),
        name="pull",
    )(grad_upper, grad_merged, weights, weights, near, far, mean, rstd)


def local(
    hidden_in, norm_gain, norm_shift, qkv_weight, qkv_bias, proj_weight, proj_bias,
    up_weight, up_bias, down_weight, down_bias, segment_ids, positions, cotangent,
):
    xh, core, xl = lax.axis_index("xh"), lax.axis_index("core"), lax.axis_index("xl")
    place = 2 * xh + xl
    hidden_own = hidden_in.reshape(128, D)
    cot_own = cotangent.reshape(128, D)

    parts = exchange4(deal(2 * xh + core, xl, up_weight, qkv_weight))
    down_part = lax.dynamic_slice_in_dim(down_weight, xl * 64, 64, 0)
    proj_part = rehome(lax.dynamic_slice_in_dim(proj_weight, xl * 16, 16, 0))
    proj_part = proj_part.reshape(16, 8, 256).swapaxes(0, 1).reshape(128, 256)
    send = jnp.concatenate(
        [
            parts[:, :1024],
            down_part[:, :1024],
            down_part[:, 1024:],
            jnp.concatenate([parts[:, 1024:], proj_part], axis=1),
        ]
    )
    weights = gather_plane(send)

    small = jnp.concatenate([norm_gain, norm_shift, proj_bias, down_bias, qkv_bias, up_bias])[None]
    hidden_turned = owner_order(hidden_own)
    marks = jnp.stack(
        [positions.reshape(128), lax.dynamic_slice_in_dim(segment_ids.reshape(SEQ), xl * 128, 128)]
    )
    small, hidden_turned, cot_sent, marks, _ = tie(small, hidden_turned, cot_own, marks, send)
    hid_below, hid_above = ring_first(hidden_turned)
    small = gather_step(small, 0)
    small, hid_below, hid_above = tie(small, hid_below, hid_above)
    hid_low, hid_high = ring_second(hid_below, hid_above)
    small = gather_step(small, 1)
    small, hid_low, hid_high, cot_sent = tie(small, hid_low, hid_high, cot_sent)
    hid = jnp.concatenate([hidden_turned, hid_above, hid_low, hid_high, hid_below])
    hid_far = shift(hid, "core", 1)
    cot_below, cot_above = ring_first(cot_sent)
    small = gather_step(small, 2)
    small, marks, cot_below, cot_above = tie(small, marks, cot_below, cot_above)
    cot_low, cot_high = ring_second(cot_below, cot_above)
    small = gather_step(small, 3)
    small, marks, cot_low, cot_high = tie(small, marks, cot_low, cot_high)
    cot = jnp.concatenate([cot_sent, cot_above, cot_low, cot_high, cot_below])
    cot_far = shift(cot, "core", 1)
    small = gather_step(small, 4)
    marks = pair_gather(marks, "xl")
    small, marks = tie(small, marks)
    small = gather_step(small, 5).astype(F32)
    marks = pair_gather(marks, "xh").reshape(4, 2, 128)
    marks = jnp.stack([pick(marks, (place + k) % 4) for k in range(4)])
    marks = jnp.stack([marks, shift(marks, "core", 1)]).transpose(2, 0, 1, 3).reshape(2, TOKENS)
    position_all, segment_all = marks[0], marks[1]

    gain = owner_order(small[:, :32].reshape(D))
    shift_row = owner_order(small[:, 32:64].reshape(D))
    out_bias = (small[:, 64:96] + small[:, 96:128]).reshape(D)
    qkv_b = small[:, 128:224].reshape(3, 2, 2, 2, 256)[:, xh, core, xl].reshape(1, 768)
    up_b = small[:, 224:352].reshape(2, 16, 2, 128)[xh, :, core]
    up_b = lax.dynamic_slice_in_dim(up_b, xl * 64, 64, 1).reshape(1, 1024)
    normed, turned, mean, rstd = norm(hid, hid_far, gain, shift_row)

    lane = jnp.arange(128) % HD
    freqs = 10000.0 ** (-(lane % 16).astype(F32) * (2.0 / ROT))
    angles = position_all.astype(F32)[:, None] * freqs
    cosine = jnp.where(lane < ROT, jnp.cos(angles), 1.0)
    sine = jnp.sin(angles)
    sin1 = jnp.where(lane < 16, sine, 0.0)
    sin2 = jnp.where((lane >= 16) & (lane < ROT), sine, 0.0)

    context, grad_merged, pack = heads(
        xl, normed, turned, cot, cot_far, weights, qkv_b, cosine, sin1, sin2, segment_all
    )
    active, grad_upper, pack = feed(normed, turned, cot, cot_far, weights, up_b, pack)
    back = scatter_plane_whole(pack)

    pulled, pulled_far, gain_sum, shift_sum, up_sum, qkv_sum = pull(
        grad_upper, grad_merged, weights, hid, hid_far, mean, rstd
    )
    out_sum = jnp.sum(cot_own.astype(F32), axis=0)
    qkv_full = lax.dynamic_update_slice(
        jnp.zeros((3, 2, 2, 2, 256), F32), qkv_sum.reshape(3, 1, 1, 1, 256), (0, xh, core, xl, 0)
    )
    up_full = lax.dynamic_update_slice(
        jnp.zeros((2, 16, 2, 2, 64), F32), up_sum.reshape(1, 16, 1, 1, 64), (xh, 0, core, xl, 0)
    )
    sums = jnp.concatenate(
        [plain_order(s.reshape(D)).reshape(64, 32) for s in (gain_sum, shift_sum)]
        + [out_sum.reshape(64, 32), qkv_full.reshape(64, 96), up_full.reshape(64, 128)],
        axis=1,
    )
    pulled_far = shift(pulled_far, "core", 1)
    sums = reduce_step(sums, 5)
    branch, branch_far = branch_out(context, after(active, gain_sum), weights)
    sums, branch_far, pulled_far = tie(sums, branch_far, pulled_far)
    pulled = sum_parts(pulled, pulled_far)
    low, high = fold_first(pulled)
    branch_far = shift(branch_far, "core", 1)
    sums = reduce_step(sums, 4)
    sums, branch_far, low, high = tie(sums, branch_far, low, high)
    from_below, from_above = fold_second(pulled, low, high)
    branch = sum_parts(branch, branch_far)
    low, high = fold_first(branch)
    sums = reduce_step(sums, 3)
    sums, low, high, from_below, from_above = tie(sums, low, high, from_below, from_above)
    branch_below, branch_above = fold_second(branch, low, high)
    sums = reduce_step(sums, 2)
    grad_own = pulled[0] + from_below.astype(F32) + from_above.astype(F32)

    own = owner_order(hidden_own).astype(F32)
    mean = jnp.mean(own, axis=-1, keepdims=True)
    centered = own - mean
    rstd = lax.rsqrt(jnp.mean(centered * centered, axis=-1, keepdims=True) + EPS)
    normal_own = centered * rstd
    scaled = grad_own * gain
    inner = jnp.mean(scaled * normal_own, axis=-1, keepdims=True)
    lifted = (scaled - jnp.mean(scaled, axis=-1, keepdims=True) - normal_own * inner) * rstd
    grad_hidden = (cot_own.astype(F32) + plain_order(lifted)).reshape(1, 128, D)

    sums, branch_below, branch_above, grad_hidden = tie(sums, branch_below, branch_above, grad_hidden)
    sums = reduce_step(reduce_step(sums, 1), 0)
    sums = (sums + shift(sums, "xl", 1))[0]
    branch = branch[0] + branch_below.astype(F32) + branch_above.astype(F32)
    block_out = hidden_own.astype(F32) + branch + out_bias
    block_out = block_out.astype(BF).reshape(1, 128, D)

    back = after(back, grad_hidden, block_out, sums)
    near, far, down_rows, proj_rows = sort(core, back)
    far = shift(far, "core", 1)
    down_rows, proj_rows = after((down_rows, proj_rows), far)
    pair = jnp.stack([near, far], axis=1)
    pieces = [pick(pair, xh)]
    for step in (1, 2, 3):
        pieces.append(shift(pick(pair, ((place + step) % 4) // 2), "x", step))
    grad_up, grad_qkv = spread(place, core, pieces)
    grad_down = pair_gather(down_rows, "xl").reshape(128, D)
    grad_proj = pair_gather(rehome(proj_rows, back=True), "xl").reshape(32, D)
    return (
        block_out,
        grad_hidden,
        sums[:32],
        sums[32:64],
        grad_qkv,
        sums[96:192],
        grad_proj.astype(F32),
        sums[64:96],
        grad_up,
        sums[192:320],
        grad_down.astype(F32),
        sums[64:96],
    )


def solution(mesh):
    cut = Mesh(mesh.devices.reshape(2, 4, 4, 2, 2), AXES)
    row, vec = P(SHARD, None), P(SHARD)
    tok = P(SHARD, "xl", None)
    return jax.shard_map(
        local,
        mesh=cut,
        in_specs=(
            tok, vec, vec, row, vec, row, vec, row, vec, row, vec, row, P(SHARD, "xl"), tok,
        ),
        out_specs=(tok, tok, vec, vec, row, vec, row, vec, row, vec, row, vec),
        check_vma=False,
    )
```

```python
import math

import jax
import jax.numpy as jnp
from jax import lax
from jax.experimental import pallas as pl
from jax.experimental.pallas import tpu as pltpu
from jax.sharding import Mesh, PartitionSpec as P

D = 2048
H = 32
HD = 64
ROT = 32
FF = 8192
SEQ = 256
SCALE = HD**-0.5
EPS = 1e-5
VMEM = 60 << 20
AXES = ("xh", "z", "y", "core", "xl")
SHARD = ("xh", "z", "y", "core")
PLANE = ("z", "y")
TOKENS = 1024
BF = jnp.bfloat16
F32 = jnp.float32


def shift(value, axis, step):
    names, size = (("xh", "xl"), 4) if axis == "x" else (axis, lax.axis_size(axis))
    return lax.ppermute(value, names, [(i, (i + step) % size) for i in range(size)])


def pick(value, index, axis=0):
    return lax.dynamic_index_in_dim(value, index, axis, keepdims=False)


def tie(*values):
    return lax.optimization_barrier(values)


def across(value, step):
    return lax.ppermute(value, ("xh", "xl"), [(i, i ^ step) for i in range(4)])


def ring_first(value):
    return shift(value, "x", 1), shift(value, "x", -1)


def ring_second(below, above):
    return shift(below[:64], "x", 1), shift(above[64:], "x", -1)


def fold_first(parts):
    far = parts[2].astype(BF)
    return shift(far[:64], "x", 1), shift(far[64:], "x", -1)


def fold_second(parts, low, high):
    after_me = jnp.concatenate([parts[1][:64] + low.astype(F32), parts[1][64:]]).astype(BF)
    before_me = jnp.concatenate([parts[3][:64], parts[3][64:] + high.astype(F32)]).astype(BF)
    return shift(after_me, "x", 1), shift(before_me, "x", -1)


def sum_parts(near, other):
    near, other = near.reshape(4, 128, D), other.reshape(4, 128, D)
    return [near[k].astype(F32) + other[k].astype(F32) for k in range(4)]


def exchange4(parts):
    xh, core = lax.axis_index("xh"), lax.axis_index("core")
    rel = [parts[0]]
    for turn in (1, 2, 3):
        rel.append(lax.ppermute(parts[turn], ("xh", "core"), [(i, i ^ turn) for i in range(4)]))
    me = 2 * xh + core
    rel = jnp.stack(rel)
    return jnp.concatenate([pick(rel, me ^ source) for source in range(4)])


def pair_gather(value, axis):
    me = lax.axis_index(axis)
    rel = jnp.stack([value, shift(value, axis, 1)])
    return jnp.where(me == 0, rel, rel[::-1])


def gather_plane(value):
    return lax.all_gather(value, PLANE, axis=0, tiled=False)


def scatter_plane_whole(value):
    flat = value.reshape(-1, value.shape[-1])
    return lax.psum_scatter(flat, PLANE, scatter_dimension=0, tiled=True)


STEPS = (("core", 1), ("y", 1), ("y", 2), ("z", 1), ("z", 2), ("xh", 1))


def toward(value, axis, bit):
    size = lax.axis_size(axis)
    return lax.ppermute(value, axis, [(i, i ^ bit) for i in range(size)])


def gather_step(value, step):
    axis, bit = STEPS[step]
    other = toward(value, axis, bit)
    high = (lax.axis_index(axis) & bit) != 0
    return jnp.concatenate([jnp.where(high, other, value), jnp.where(high, value, other)])


def reduce_step(value, step):
    axis, bit = STEPS[step]
    parts = value.reshape(2, value.shape[0] // 2, value.shape[1])
    mine = jnp.where((lax.axis_index(axis) & bit) != 0, 1, 0)
    return pick(parts, mine) + toward(pick(parts, 1 - mine), axis, bit)


def rehome(value, back=False, other=False):
    pairs = []
    for z in range(4):
        for y in range(4):
            for core in range(2):
                for xl in range(2):
                    owner = ((z * 4 + y) * 2 + core) * 2 + (xl ^ 1 if other else xl)
                    user = ((y * 4 + 2 * core + xl) * 2 + z // 2) * 2 + z % 2
                    pairs.append((user, owner) if back else (owner, user))
    return lax.ppermute(value, ("z", "y", "core", "xl"), pairs)


def owner_order(vector):
    lead = vector.shape[:-1]
    size = vector.shape[-1] // 32
    return jnp.swapaxes(vector.reshape(*lead, 2, 16, size), -3, -2).reshape(*lead, -1)


def plain_order(vector):
    lead = vector.shape[:-1]
    size = vector.shape[-1] // 32
    return jnp.swapaxes(vector.reshape(*lead, 16, 2, size), -3, -2).reshape(*lead, -1)


def dot(left, right):
    return jnp.dot(left, right, preferred_element_type=F32)


def dot_rows(left, right):
    return lax.dot_general(left, right, (((0,), (0,)), ((), ())), preferred_element_type=F32)


def dot_cols(left, right):
    return lax.dot_general(left, right, (((1,), (1,)), ((), ())), preferred_element_type=F32)


def deal_body(place_ref, up_ref, qkv_ref, out_ref):
    me, xl = place_ref[0], place_ref[1]
    lane = lax.broadcasted_iota(jnp.int32, (32, 128), 1)
    for turn in range(4):
        target = me ^ turn
        xh, core = lax.div(target, 2), lax.rem(target, 2)
        for pair in range(8):
            start = xh * 4096 + core * 128 + pair * 512
            left = up_ref[:, pl.ds(pl.multiple_of(start, 128), 128)].astype(F32)
            right = up_ref[:, pl.ds(pl.multiple_of(start + 256, 128), 128)].astype(F32)
            left = jnp.where(xl == 0, left, pltpu.roll(left, 64, 1))
            right = jnp.where(xl == 0, pltpu.roll(right, 64, 1), right)
            both = jnp.where(lane < 64, left, right).astype(BF)
            out_ref[turn, :, pair * 128 : (pair + 1) * 128] = both
        for block in range(3):
            start = block * D + xh * 1024 + core * 512 + xl * 256
            out_ref[turn, :, 1024 + block * 256 : 1280 + block * 256] = qkv_ref[
                :, pl.ds(pl.multiple_of(start, 256), 256)
            ]


def deal(me, xl, up, qkv):
    vmem = pl.BlockSpec(memory_space=pltpu.VMEM)
    return pl.pallas_call(
        deal_body,
        in_specs=[pl.BlockSpec(memory_space=pltpu.SMEM), vmem, vmem],
        out_specs=vmem,
        out_shape=jax.ShapeDtypeStruct((4, 32, 1792), BF),
        name="deal",
    )(jnp.stack([me, xl]).astype(jnp.int32), up, qkv)


def spread_body(place_ref, *refs):
    pieces, other_ref, down_own, proj_refs = refs[:4], refs[4], refs[5], refs[6:8]
    up_ref, qkv_ref, down_ref, proj_ref, held = refs[8:]
    place, core, xl = place_ref[0], place_ref[1], place_ref[2]
    for step in range(4):
        held[place ^ step, core] = pieces[step][:64]
        held[place ^ step, 1 - core] = other_ref[step]
    rows = pl.ds(pl.multiple_of(xl * 64, 64), 64)
    down_ref[rows, :1024] = down_own[:64].astype(F32)
    down_ref[rows, 1024:] = down_own[64:].astype(F32)
    rows = pl.ds(pl.multiple_of((1 - xl) * 64, 64), 64)
    down_ref[rows, :1024] = pieces[1][128:192].astype(F32)
    down_ref[rows, 1024:] = pieces[1][192:].astype(F32)
    for side in range(2):
        start = pl.multiple_of((xl ^ side) * 16, 16)
        proj_ref[pl.ds(start, 16), :] = proj_refs[side][...].astype(F32)
    for xh in range(2):
        for unit in range(16):
            for side in range(2):
                block = [
                    held[2 * xh + x, side, :32, unit * 64 : (unit + 1) * 64].astype(F32) for x in range(2)
                ]
                start = xh * 4096 + unit * 256 + side * 128
                up_ref[:, start : start + 128] = jnp.concatenate(block, axis=1)
        for side in range(2):
            for x in range(2):
                for block in range(3):
                    start = block * D + xh * 1024 + side * 512 + x * 256
                    qkv_ref[:, start : start + 256] = held[
                        2 * xh + x, side, 32:, block * 256 : (block + 1) * 256
                    ].astype(F32)


def spread(scalars, pieces, other, down, proj):
    vmem = pl.BlockSpec(memory_space=pltpu.VMEM)
    return pl.pallas_call(
        spread_body,
        in_specs=[pl.BlockSpec(memory_space=pltpu.SMEM)] + [vmem] * 8,
        out_specs=[vmem] * 4,
        out_shape=[
            jax.ShapeDtypeStruct((32, FF), F32),
            jax.ShapeDtypeStruct((32, 3 * D), F32),
            jax.ShapeDtypeStruct((128, D), F32),
            jax.ShapeDtypeStruct((32, D), F32),
        ],
        scratch_shapes=[pltpu.VMEM((4, 2, 64, 1024), BF)],
        name="spread",
    )(scalars, *pieces, other, down, *proj)


def sort_body(place_ref, in_ref, *refs):
    down_ref, proj_ref = refs[4], refs[5]
    place, core = place_ref[0], place_ref[1]
    for step in range(4):
        xh = lax.div(place ^ step, 2)
        for side in range(2):
            start = pl.multiple_of(xh * 64 + (core ^ side) * 32, 32)
            at = side * 64
            refs[step][at : at + 32] = in_ref[pl.ds(start, 32), :]
            refs[step][at + 32 : at + 64] = in_ref[pl.ds(pl.multiple_of(start + 256, 32), 32), :]
    refs[1][128:] = in_ref[128:256, :]
    down_ref[...] = in_ref[128:256, :]
    for block in range(8):
        proj_ref[:, block * 256 : (block + 1) * 256] = in_ref[
            256 + block * 16 : 272 + block * 16, 768:
        ]


def sort(scalars, summed):
    vmem = pl.BlockSpec(memory_space=pltpu.VMEM)
    return pl.pallas_call(
        sort_body,
        in_specs=[pl.BlockSpec(memory_space=pltpu.SMEM), vmem],
        out_specs=[vmem] * 6,
        out_shape=[
            jax.ShapeDtypeStruct((256 if step == 1 else 128, 1024), BF) for step in range(4)
        ]
        + [jax.ShapeDtypeStruct((128, 1024), BF), jax.ShapeDtypeStruct((16, D), BF)],
        name="sort",
    )(scalars, summed)


def norm_body(near_ref, far_ref, gain_ref, shift_ref, normed_ref, turned_ref, mean_ref, rstd_ref):
    hidden = jnp.where(pl.program_id(0) < 2, near_ref[...], far_ref[...]).astype(F32)
    mean = jnp.mean(hidden, axis=-1, keepdims=True)
    centered = hidden - mean
    rstd = lax.rsqrt(jnp.mean(centered * centered, axis=-1, keepdims=True) + EPS)
    normed = (centered * rstd * gain_ref[...] + shift_ref[...]).astype(BF)
    normed_ref[...] = normed
    turned_ref[...] = normed.T
    mean_ref[...] = mean
    rstd_ref[...] = rstd


def norm(near, far, gain, shift_row):
    step = 256
    row = pl.BlockSpec((step, D), lambda i: (i, 0))
    vec = pl.BlockSpec((1, D), lambda i: (0, 0))
    one = pl.BlockSpec((step, 1), lambda i: (i, 0))
    return pl.pallas_call(
        norm_body,
        grid=(TOKENS // step,),
        in_specs=[
            pl.BlockSpec((step, D), lambda i: (jnp.minimum(i, 1), 0)),
            pl.BlockSpec((step, D), lambda i: (jnp.maximum(i - 2, 0), 0)),
            vec,
            vec,
        ],
        out_specs=[row, pl.BlockSpec((D, step), lambda i: (0, i)), one, one],
        out_shape=[
            jax.ShapeDtypeStruct((TOKENS, D), BF),
            jax.ShapeDtypeStruct((D, TOKENS), BF),
            jax.ShapeDtypeStruct((TOKENS, 1), F32),
            jax.ShapeDtypeStruct((TOKENS, 1), F32),
        ],
        compiler_params=pltpu.CompilerParams(vmem_limit_bytes=VMEM),
        cost_estimate=pl.CostEstimate(flops=20 << 20, bytes_accessed=12 << 20, transcendentals=0),
        name="norm",
    )(near, far, gain.reshape(1, D), shift_row.reshape(1, D))


def work_body(odd_ref, normed_hbm, turned_hbm, near_hbm, far_hbm, weights_hbm, bias_ref, up_bias_ref,
              cos_hbm, sin1_hbm, sin2_hbm, row_ref, col_hbm, ctx_hbm, out_hbm, act_hbm, grad_hbm, pack_hbm,
              cos_ref, sin1_ref, sin2_ref, col_ref, normed, turned, cot, ctx_ref, out_ref, weights, proj, merged, queries, keys, values, grads, mask, raw, pulled,
               probs, slopes, back_q, back_k, packed, sem, out_sems,
              up, down, act, units, upper_ref, slope_ref, up_out, down_out,
              act_sems, grad_sems, up_sems, down_sems):
    width = 4 * HD
    half = ROT // 2
    loads = [
        pltpu.make_async_copy(weights_hbm.at[:, pl.ds(256, 128), :], weights, sem.at[0]),
        pltpu.make_async_copy(normed_hbm, normed, sem.at[1]),
        pltpu.make_async_copy(near_hbm, cot.at[pl.ds(0, 512)], sem.at[2]),
        pltpu.make_async_copy(far_hbm, cot.at[pl.ds(512, 512)], sem.at[3]),
        pltpu.make_async_copy(turned_hbm, turned, sem.at[4]),
        pltpu.make_async_copy(cos_hbm, cos_ref, sem.at[5]),
        pltpu.make_async_copy(sin1_hbm, sin1_ref, sem.at[6]),
        pltpu.make_async_copy(sin2_hbm, sin2_ref, sem.at[7]),
        pltpu.make_async_copy(col_hbm, col_ref, sem.at[8]),
    ]
    for place in (0, 1, 5, 6, 7, 8, 2, 3, 4):
        loads[place].start()
    up_load = pltpu.make_async_copy(weights_hbm.at[:, pl.ds(0, 128), :], up, sem.at[9])
    down_load = pltpu.make_async_copy(weights_hbm.at[:, pl.ds(128, 128), :], down, sem.at[10])
    up_load.start()
    down_load.start()
    odd = odd_ref[0]
    for k in range(2):
        probs[k, :128, 128:] = jnp.zeros((128, 128), BF)
        slopes[k, :128, 128:] = jnp.zeros((128, 128), BF)

    def sides(item):
        pair, base = lax.rem(item, 2), lax.div(item, 2) * 512
        first = pl.multiple_of(base + lax.rem(2 * pair + 3 * odd, 4) * 128, 128)
        second = pl.multiple_of(base + lax.rem(2 * pair + 3 * odd + 1, 4) * 128, 128)
        return first, second

    for place in (0, 1, 5, 6, 7, 8):
        loads[place].wait()
    for block in range(8):
        proj[:, block * 256 : (block + 1) * 256] = weights[
            :, block * 16 : (block + 1) * 16, 768:
        ].reshape(256, 256)

    @pl.loop(0, 4)
    def _(step):
        rows = pl.ds(pl.multiple_of(step * 256, 256), 256)
        merged[...] = dot(normed[rows, :], weights[:, :, :768].reshape(D, 768)) + bias_ref[...]
        @pl.loop(0, 8)
        def _(part):
            here = pl.ds(pl.multiple_of(part * 32, 32), 32)
            there = pl.ds(pl.multiple_of(step * 256 + part * 32, 32), 32)
            cosine, sin1, sin2 = cos_ref[there, :], sin1_ref[there, :], sin2_ref[there, :]
            for pair in range(2):
                for ref, base in ((queries, 0), (keys, width)):
                    value = merged[here, base + pair * 128 : base + (pair + 1) * 128]
                    value = (
                        value * cosine
                        - pltpu.roll(value, 128 - half, 1) * sin1
                        + pltpu.roll(value, half, 1) * sin2
                    )
                    ref[pair, there, :] = (value * SCALE if base == 0 else value).astype(BF)
                start = 2 * width + pair * 128
                values[pair, there, :] = merged[here, start : start + 128].astype(BF)

    loads[2].wait()
    loads[3].wait()

    @pl.loop(0, 2)
    def _(step):
        rows = pl.ds(pl.multiple_of(step * 512, 512), 512)
        pulls = dot_cols(cot[rows, :], proj[...]).astype(BF)
        for pair in range(2):
            grads[pair, rows, :] = pulls[:, pair * 128 : (pair + 1) * 128]

    lane = lax.broadcasted_iota(jnp.int32, (SEQ, 128), 1)
    low = lane < HD

    @pl.loop(0, 4)
    def _(item):
        first, second = sides(item)
        segment = row_ref[item]
        for start in range(0, SEQ, 64):
            side = first if start < 128 else second
            rows = lax.broadcasted_iota(jnp.int32, (64, SEQ), 0) + start
            cols = lax.broadcasted_iota(jnp.int32, (64, SEQ), 1)
            own = col_ref[pl.ds(pl.multiple_of(side + start % 128, 64), 64), :]
            allowed = (cols <= rows) & (own == segment)
            mask[start : start + 64, :] = jnp.where(allowed, 0.0, -1e30)

        for pair in range(2):

            def load(ref):
                return jnp.concatenate([ref[pair, pl.ds(first, 128), :], ref[pair, pl.ds(second, 128), :]])

            query, key, value, grad = load(queries), load(keys), load(values), load(grads)
            for k in range(2):
                own = low if k == 0 else ~low
                raw[k] = dot_cols(jnp.where(own, query, 0), key)
                pulled[k] = dot_cols(jnp.where(own, grad, 0), value)
            for k in range(2):
                for start in range(0, SEQ, 32):
                    size = 128 if start < 128 else SEQ
                    rows = slice(start, start + 32)
                    scores = raw[k, rows, :size] + mask[rows, :size]
                    top = jnp.max(scores, axis=-1, keepdims=True)
                    expo = jnp.exp(scores - top)
                    prob = expo * (1.0 / jnp.sum(expo, axis=-1, keepdims=True))
                    probs[k, rows, :size] = prob.astype(BF)
                    grad_prob = pulled[k, rows, :size]
                    inner = jnp.sum(prob * grad_prob, axis=-1, keepdims=True)
                    slopes[k, rows, :size] = (prob * (grad_prob - inner)).astype(BF)
            context = jnp.where(low, dot(probs[0], value), dot(probs[1], value)).astype(BF)
            grad_v = jnp.where(low, dot_rows(probs[0], grad), dot_rows(probs[1], grad)).astype(BF)
            back_q[...] = SCALE * jnp.where(low, dot(slopes[0], key), dot(slopes[1], key))
            back_k[...] = jnp.where(low, dot_rows(slopes[0], query), dot_rows(slopes[1], query))
            lanes = slice(pair * 128, (pair + 1) * 128)
            for at, side in ((0, first), (128, second)):
                rows = pl.ds(side, 128)
                ctx_ref[rows, lanes] = context[at : at + 128]
                out_ref[rows, 2 * width + pair * 128 : 2 * width + (pair + 1) * 128] = grad_v[at : at + 128]
                for start in range(0, 128, 32):
                    there = pl.ds(pl.multiple_of(side + start, 32), 32)
                    cosine, sin1, sin2 = cos_ref[there, :], sin1_ref[there, :], sin2_ref[there, :]
                    for ref, base in ((back_q, 0), (back_k, width)):
                        turned_back = ref[at + start : at + start + 32, :]
                        turned_back = (
                            turned_back * cosine
                            + pltpu.roll(turned_back, 128 - half, 1) * sin1
                            - pltpu.roll(turned_back, half, 1) * sin2
                        )
                        out_ref[there, base + pair * 128 : base + (pair + 1) * 128] = turned_back.astype(BF)

    def store(step):
        owners = pl.ds(step * 2, 2)
        return pltpu.make_async_copy(
            packed.at[owners], pack_hbm.at[owners, pl.ds(256, 128), :], out_sems.at[step]
        )

    ctx_store = pltpu.make_async_copy(ctx_ref, ctx_hbm, sem.at[0])
    out_store = pltpu.make_async_copy(out_ref, out_hbm, sem.at[1])
    ctx_store.start()
    out_store.start()

    total = dot_rows(ctx_ref[...], cot[...]).astype(BF)
    for block in range(8):
        packed[:, block * 16 : (block + 1) * 16, 768:] = total[
            :, block * 256 : (block + 1) * 256
        ].reshape(16, 16, 256)
    loads[4].wait()

    @pl.loop(0, 8)
    def _(step):
        rows = pl.ds(pl.multiple_of(step * 256, 256), 256)
        total = dot(turned[rows, :], out_ref[...]).astype(BF)
        packed[pl.ds(step * 2, 2), :, :768] = total.reshape(2, 128, 768)
        store(step).start()

    def act_store(step):
        rows = pl.ds(pl.multiple_of(step * 256, 256), 256)
        return pltpu.make_async_copy(act.at[rows, :], act_hbm.at[rows, :], act_sems.at[step])

    def grad_store(step):
        rows = pl.ds(pl.multiple_of(step * 256, 256), 256)
        return pltpu.make_async_copy(units.at[rows, :], grad_hbm.at[rows, :], grad_sems.at[step])

    def up_store(step):
        owners = pl.ds(step * 2, 2)
        return pltpu.make_async_copy(
            up_out.at[owners], pack_hbm.at[owners, pl.ds(0, 128), :], up_sems.at[step]
        )

    def down_store(step):
        owners = pl.ds(step * 4, 4)
        return pltpu.make_async_copy(
            down_out.at[owners], pack_hbm.at[owners, pl.ds(128, 128), :], down_sems.at[step]
        )

    root = math.sqrt(2.0 / math.pi)
    up_load.wait()

    @pl.loop(0, 4)
    def _(step):
        rows = pl.ds(pl.multiple_of(step * 256, 256), 256)
        upper_ref[rows, :] = dot(normed[rows, :], up[...].reshape(D, 1024)) + up_bias_ref[...]

    down_load.wait()

    @pl.loop(0, 4)
    def _(step):
        rows = pl.ds(pl.multiple_of(step * 256, 256), 256)
        slope_ref[...] = dot_cols(cot[rows, :1024], down[:, :64].reshape(1024, 1024)) + dot_cols(
            cot[rows, 1024:], down[:, 64:].reshape(1024, 1024)
        )

        @pl.loop(0, 16)
        def _(part):
            here = pl.ds(pl.multiple_of(part * 16, 16), 16)
            there = pl.ds(pl.multiple_of(step * 256 + part * 16, 16), 16)
            for side in range(2):
                lanes = slice(side * 512, side * 512 + 512)
                upper = upper_ref[there, lanes]
                square = upper * upper
                bend = jnp.tanh(upper * (root + (root * 0.044715) * square))
                half = 0.5 + 0.5 * bend
                slope = half + upper * (0.5 - 0.5 * (bend * bend)) * (root + (root * 3 * 0.044715) * square)
                act[there, lanes] = (upper * half).astype(BF)
                units[there, lanes] = (slope_ref[here, lanes] * slope).astype(BF)

        act_store(step).start()
        grad_store(step).start()

    @pl.loop(0, 8)
    def _(step):
        rows = pl.ds(pl.multiple_of(step * 256, 256), 256)
        total = dot(turned[rows, :], units[...]).astype(BF)
        up_out[pl.ds(step * 2, 2)] = total.reshape(2, 128, 1024)
        up_store(step).start()

    @pl.loop(0, 4)
    def _(step):
        lanes = pl.ds(pl.multiple_of(step * 256, 256), 256)
        total = dot_rows(act[:, lanes], cot[...]).astype(BF)
        down_out[pl.ds(step * 4, 4), :64] = total[:, :1024].reshape(4, 64, 1024)
        down_out[pl.ds(step * 4, 4), 64:] = total[:, 1024:].reshape(4, 64, 1024)
        down_store(step).start()

    @pl.loop(0, 4)
    def _(step):
        act_store(step).wait()
        grad_store(step).wait()
        down_store(step).wait()

    @pl.loop(0, 8)
    def _(step):
        up_store(step).wait()

    ctx_store.wait()
    out_store.wait()

    @pl.loop(0, 8)
    def _(step):
        store(step).wait()


def work(odd, normed, turned, near, far, weights, bias, up_bias, cosine, sin1, sin2, segment):
    blocks = segment.reshape(2, 4, 128)
    rows = jnp.where(odd == 0, blocks, jnp.roll(blocks, 1, axis=1)).reshape(4, 1, SEQ)
    vmem, hbm = pl.BlockSpec(memory_space=pltpu.VMEM), pl.BlockSpec(memory_space=pltpu.HBM)
    table = pltpu.VMEM((TOKENS, 128), F32)
    head_b = pltpu.VMEM((2, TOKENS, 128), BF)
    head_f = pltpu.VMEM((SEQ, 128), F32)
    slab = pltpu.VMEM((16, 128, 1024), BF)
    square = pltpu.VMEM((TOKENS, 1024), BF)
    return pl.pallas_call(
        work_body,
        in_specs=[pl.BlockSpec(memory_space=pltpu.SMEM)]
        + [hbm] * 5
        + [vmem] * 2
        + [hbm] * 3
        + [vmem, hbm],
        out_specs=[hbm] * 5,
        out_shape=[
            jax.ShapeDtypeStruct((TOKENS, 4 * HD), BF),
            jax.ShapeDtypeStruct((TOKENS, 12 * HD), BF),
            jax.ShapeDtypeStruct((TOKENS, 1024), BF),
            jax.ShapeDtypeStruct((TOKENS, 1024), BF),
            jax.ShapeDtypeStruct((16, 384, 1024), BF),
        ],
        scratch_shapes=[
            table,
            table,
            table,
            pltpu.VMEM((TOKENS, 1), jnp.int32),
            pltpu.VMEM((TOKENS, D), BF),
            pltpu.VMEM((D, TOKENS), BF),
            pltpu.VMEM((TOKENS, D), BF),
            pltpu.VMEM((TOKENS, 4 * HD), BF),
            pltpu.VMEM((TOKENS, 12 * HD), BF),
            slab,
            pltpu.VMEM((256, D), BF),
            pltpu.VMEM((256, 12 * HD), F32),
            head_b,
            head_b,
            head_b,
            head_b,
            pltpu.VMEM((SEQ, SEQ), F32),
            pltpu.VMEM((2, SEQ, SEQ), F32),
            pltpu.VMEM((2, SEQ, SEQ), F32),
            pltpu.VMEM((2, SEQ, SEQ), BF),
            pltpu.VMEM((2, SEQ, SEQ), BF),
            head_f,
            head_f,
            slab,
            pltpu.SemaphoreType.DMA((11,)),
            pltpu.SemaphoreType.DMA((8,)),
            slab,
            slab,
            square,
            square,
            pltpu.VMEM((TOKENS, 1024), F32),
            pltpu.VMEM((256, 1024), F32),
            slab,
            slab,
            pltpu.SemaphoreType.DMA((4,)),
            pltpu.SemaphoreType.DMA((4,)),
            pltpu.SemaphoreType.DMA((8,)),
            pltpu.SemaphoreType.DMA((4,)),
        ],
        compiler_params=pltpu.CompilerParams(vmem_limit_bytes=VMEM),
        cost_estimate=pl.CostEstimate(
            flops=30 << 30, bytes_accessed=64 << 20, transcendentals=2 * TOKENS * 1024
        ),
        name="work",
    )(
        odd.reshape(1), normed, turned, near, far, weights, bias, up_bias, cosine, sin1, sin2, rows,
        segment.reshape(TOKENS, 1),
    )


def branch_body(context_ref, proj_ref, act_ref, down_ref, near_ref, far_ref):
    total = dot(act_ref[...], down_ref[...].reshape(1024, 256))
    total = (total + dot(context_ref[...], proj_ref[...].reshape(256, 256))).astype(BF)
    near_ref[...] = total[:512]
    far_ref[...] = total[512:]


def branch_out(context, active, weights):
    return pl.pallas_call(
        branch_body,
        grid=(8,),
        in_specs=[
            pl.BlockSpec((TOKENS, 256), lambda n: (0, 0), pipeline_mode=pl.Buffered(1)),
            pl.BlockSpec((16, 16, 256), lambda n: (0, 16 + n, 3)),
            pl.BlockSpec((TOKENS, 1024), lambda n: (0, 0), pipeline_mode=pl.Buffered(1)),
            pl.BlockSpec((16, 64, 256), lambda n: (0, 2 + n // 4, n % 4)),
        ],
        out_specs=[pl.BlockSpec((512, 256), lambda n: (0, n))] * 2,
        out_shape=[jax.ShapeDtypeStruct((512, D), BF)] * 2,
        compiler_params=pltpu.CompilerParams(vmem_limit_bytes=VMEM),
        cost_estimate=pl.CostEstimate(
            flops=2 * TOKENS * D * 1280, bytes_accessed=12 << 20, transcendentals=0
        ),
        name="branch",
    )(context, weights, active, weights)


def pull_body(grad_ref, merged_ref, up_ref, qkv_ref, hid_near_ref, hid_far_ref, mean_ref, rstd_ref,
              near_ref, far_ref, gain_ref, shift_ref, up_ref_sum, qkv_ref_sum):
    total = dot_cols(grad_ref[...], up_ref[...].reshape(256, 1024))
    total = total + dot_cols(merged_ref[...], qkv_ref[...].reshape(256, 1024)[:, :768])
    near_ref[...] = total[:512].astype(BF)
    far_ref[...] = total[512:].astype(BF)
    hidden = jnp.concatenate([hid_near_ref[...], hid_far_ref[...]]).astype(F32)
    normal = (hidden - mean_ref[...]) * rstd_ref[...]
    gain_ref[...] = jnp.sum(total * normal, axis=0, keepdims=True)
    shift_ref[...] = jnp.sum(total, axis=0, keepdims=True)

    @pl.when(pl.program_id(0) == 0)
    def _():
        ones = jnp.ones((16, TOKENS), BF)
        up_ref_sum[...] = dot(ones, grad_ref[...])[:1]
        qkv_ref_sum[...] = dot(ones, merged_ref[...])[:1]


def pull(grad_upper, grad_merged, weights, near, far, mean, rstd):
    def whole(width):
        return pl.BlockSpec((TOKENS, width), lambda n: (0, 0), pipeline_mode=pl.Buffered(1))

    half = pl.BlockSpec((512, 256), lambda n: (0, n))
    vec = pl.BlockSpec((1, 256), lambda n: (0, n))
    return pl.pallas_call(
        pull_body,
        grid=(8,),
        in_specs=[
            whole(1024),
            whole(768),
            pl.BlockSpec((2, 128, 1024), lambda n: (n, 0, 0)),
            pl.BlockSpec((2, 128, 1024), lambda n: (n, 2, 0)),
            half,
            half,
            whole(1),
            whole(1),
        ],
        out_specs=[half] * 2
        + [vec, vec, pl.BlockSpec((1, 1024), lambda n: (0, 0)), pl.BlockSpec((1, 768), lambda n: (0, 0))],
        out_shape=[
            jax.ShapeDtypeStruct((512, D), BF),
            jax.ShapeDtypeStruct((512, D), BF),
            jax.ShapeDtypeStruct((1, D), F32),
            jax.ShapeDtypeStruct((1, D), F32),
            jax.ShapeDtypeStruct((1, 1024), F32),
            jax.ShapeDtypeStruct((1, 768), F32),
        ],
        compiler_params=pltpu.CompilerParams(vmem_limit_bytes=VMEM),
        cost_estimate=pl.CostEstimate(
            flops=2 * TOKENS * D * 1792, bytes_accessed=16 << 20, transcendentals=0
        ),
        name="pull",
    )(grad_upper, grad_merged, weights, weights, near, far, mean, rstd)


def local(
    hidden_in, norm_gain, norm_shift, qkv_weight, qkv_bias, proj_weight, proj_bias,
    up_weight, up_bias, down_weight, down_bias, segment_ids, positions, cotangent,
):
    xh, core, xl = lax.axis_index("xh"), lax.axis_index("core"), lax.axis_index("xl")
    place = 2 * xh + xl
    scalars = jnp.stack([place, core, xl]).astype(jnp.int32)
    hidden_own = hidden_in.reshape(128, D)
    cot_own = cotangent.reshape(128, D)

    parts = exchange4(deal(2 * xh + core, xl, up_weight, qkv_weight))
    down_part = lax.dynamic_slice_in_dim(down_weight, xl * 64, 64, 0)
    proj_part = rehome(lax.dynamic_slice_in_dim(proj_weight, xl * 16, 16, 0))
    proj_part = proj_part.reshape(16, 8, 256).swapaxes(0, 1).reshape(128, 256)
    send = jnp.concatenate(
        [
            parts[:, :1024],
            down_part[:, :1024],
            down_part[:, 1024:],
            jnp.concatenate([parts[:, 1024:], proj_part], axis=1),
        ]
    )
    weights = gather_plane(send)

    small = jnp.concatenate([norm_gain, norm_shift, proj_bias, down_bias, qkv_bias, up_bias])[None]
    hidden_turned = owner_order(hidden_own)
    marks = jnp.stack(
        [positions.reshape(128), lax.dynamic_slice_in_dim(segment_ids.reshape(SEQ), xl * 128, 128)]
    )
    small, hidden_turned, cot_sent, marks, _ = tie(small, hidden_turned, cot_own, marks, send)
    hid_below, hid_above = ring_first(hidden_turned)
    small = gather_step(small, 0)
    small, hid_below, hid_above = tie(small, hid_below, hid_above)
    hid_low, hid_high = ring_second(hid_below, hid_above)
    small = gather_step(small, 1)
    small, hid_low, hid_high, cot_sent = tie(small, hid_low, hid_high, cot_sent)
    hid = jnp.concatenate([hidden_turned, hid_above, hid_low, hid_high, hid_below])
    hid_far = shift(hid, "core", 1)
    cot_below, cot_above = ring_first(cot_sent)
    small = gather_step(small, 2)
    small, marks, cot_below, cot_above = tie(small, marks, cot_below, cot_above)
    cot_low, cot_high = ring_second(cot_below, cot_above)
    small = gather_step(small, 3)
    small, marks, cot_low, cot_high = tie(small, marks, cot_low, cot_high)
    cot = jnp.concatenate([cot_sent, cot_above, cot_low, cot_high, cot_below])
    cot_far = shift(cot, "core", 1)
    small = gather_step(small, 4)
    marks = pair_gather(marks, "xl")
    small, marks = tie(small, marks)
    small = gather_step(small, 5).astype(F32)
    marks = pair_gather(marks, "xh").reshape(4, 2, 128)
    marks = jnp.stack([pick(marks, (place + k) % 4) for k in range(4)])
    marks = jnp.stack([marks, shift(marks, "core", 1)]).transpose(2, 0, 1, 3).reshape(2, TOKENS)
    position_all, segment_all = marks[0], marks[1]

    gain = owner_order(small[:, :32].reshape(D))
    shift_row = owner_order(small[:, 32:64].reshape(D))
    out_bias = (small[:, 64:96] + small[:, 96:128]).reshape(D)
    qkv_b = small[:, 128:224].reshape(3, 2, 2, 2, 256)[:, xh, core, xl].reshape(1, 768)
    up_b = small[:, 224:352].reshape(2, 16, 2, 128)[xh, :, core]
    up_b = lax.dynamic_slice_in_dim(up_b, xl * 64, 64, 1).reshape(1, 1024)
    normed, turned, mean, rstd = norm(hid, hid_far, gain, shift_row)

    lane = jnp.arange(128) % HD
    freqs = 10000.0 ** (-(lane % 16).astype(F32) * (2.0 / ROT))
    angles = position_all.astype(F32)[:, None] * freqs
    cosine = jnp.where(lane < ROT, jnp.cos(angles), 1.0)
    sine = jnp.sin(angles)
    sin1 = jnp.where(lane < 16, sine, 0.0)
    sin2 = jnp.where((lane >= 16) & (lane < ROT), sine, 0.0)

    context, grad_merged, active, grad_upper, pack = work(
        xl, normed, turned, cot, cot_far, weights, qkv_b, up_b, cosine, sin1, sin2, segment_all
    )
    back = scatter_plane_whole(pack)

    pulled, pulled_far, gain_sum, shift_sum, up_sum, qkv_sum = pull(
        grad_upper, grad_merged, weights, hid, hid_far, mean, rstd
    )
    out_sum = jnp.sum(cot_own.astype(F32), axis=0)
    qkv_full = lax.dynamic_update_slice(
        jnp.zeros((3, 2, 2, 2, 256), F32), qkv_sum.reshape(3, 1, 1, 1, 256), (0, xh, core, xl, 0)
    )
    up_full = lax.dynamic_update_slice(
        jnp.zeros((2, 16, 2, 2, 64), F32), up_sum.reshape(1, 16, 1, 1, 64), (xh, 0, core, xl, 0)
    )
    sums = jnp.concatenate(
        [plain_order(s.reshape(D)).reshape(64, 32) for s in (gain_sum, shift_sum)]
        + [out_sum.reshape(64, 32), qkv_full.reshape(64, 96), up_full.reshape(64, 128)],
        axis=1,
    )
    pulled_far = shift(pulled_far, "core", 1)
    sums = reduce_step(sums, 5)
    branch, branch_far = branch_out(context, active, weights)
    sums, branch_far, pulled_far = tie(sums, branch_far, pulled_far)
    pulled = sum_parts(pulled, pulled_far)
    low, high = fold_first(pulled)
    branch_far = shift(branch_far, "core", 1)
    sums = reduce_step(reduce_step(reduce_step(sums, 4), 3), 2)
    sums, branch_far, low, high = tie(sums, branch_far, low, high)
    from_below, from_above = fold_second(pulled, low, high)
    branch = sum_parts(branch, branch_far)
    low, high = fold_first(branch)
    sums = reduce_step(reduce_step(sums, 1), 0)
    sums = (sums + shift(sums, "xl", 1))[0]
    sums, low, high, from_below, from_above = tie(sums, low, high, from_below, from_above)
    branch_below, branch_above = fold_second(branch, low, high)
    grad_own = pulled[0] + from_below.astype(F32) + from_above.astype(F32)

    own = owner_order(hidden_own).astype(F32)
    mean = jnp.mean(own, axis=-1, keepdims=True)
    centered = own - mean
    rstd = lax.rsqrt(jnp.mean(centered * centered, axis=-1, keepdims=True) + EPS)
    normal_own = centered * rstd
    scaled = grad_own * gain
    inner = jnp.mean(scaled * normal_own, axis=-1, keepdims=True)
    lifted = (scaled - jnp.mean(scaled, axis=-1, keepdims=True) - normal_own * inner) * rstd
    grad_hidden = (cot_own.astype(F32) + plain_order(lifted)).reshape(1, 128, D)

    branch = branch[0] + branch_below.astype(F32) + branch_above.astype(F32)
    block_out = hidden_own.astype(F32) + branch + out_bias
    block_out = block_out.astype(BF).reshape(1, 128, D)

    back, grad_hidden, block_out, sums = tie(back, grad_hidden, block_out, sums)
    *pieces, down_rows, proj_rows = sort(scalars, back)
    pieces = [pieces[0]] + [across(pieces[step], step) for step in (1, 2, 3)]
    proj = (rehome(proj_rows, back=True), rehome(proj_rows, back=True, other=True))
    pieces, proj = tie(pieces, proj)
    other = shift(jnp.stack([piece[64:128] for piece in pieces]), "core", 1)
    grad_up, grad_qkv, grad_down, grad_proj = spread(scalars, pieces, other, down_rows, proj)
    return (
        block_out,
        grad_hidden,
        sums[:32],
        sums[32:64],
        grad_qkv,
        sums[96:192],
        grad_proj,
        sums[64:96],
        grad_up,
        sums[192:320],
        grad_down,
        sums[64:96],
    )


def solution(mesh):
    cut = Mesh(mesh.devices.reshape(2, 4, 4, 2, 2), AXES)
    row, vec = P(SHARD, None), P(SHARD)
    tok = P(SHARD, "xl", None)
    return jax.shard_map(
        local,
        mesh=cut,
        in_specs=(
            tok, vec, vec, row, vec, row, vec, row, vec, row, vec, row, P(SHARD, "xl"), tok,
        ),
        out_specs=(tok, tok, vec, vec, row, vec, row, vec, row, vec, row, vec),
        check_vma=False,
    )
```

```python
import math

import jax
import jax.numpy as jnp
from jax import lax
from jax.experimental import pallas as pl
from jax.experimental.pallas import tpu as pltpu
from jax.sharding import Mesh, PartitionSpec as P

D = 2048
H = 32
HD = 64
ROT = 32
FF = 8192
SEQ = 256
SCALE = HD**-0.5
EPS = 1e-5
VMEM = 60 << 20
AXES = ("xh", "z", "y", "core", "xl")
SHARD = ("xh", "z", "y", "core")
PLANE = ("z", "y")
TOKENS = 1024
BF = jnp.bfloat16
F32 = jnp.float32


def shift(value, axis, step):
    names, size = (("xh", "xl"), 4) if axis == "x" else (axis, lax.axis_size(axis))
    return lax.ppermute(value, names, [(i, (i + step) % size) for i in range(size)])


def pick(value, index, axis=0):
    return lax.dynamic_index_in_dim(value, index, axis, keepdims=False)


def tie(*values):
    return lax.optimization_barrier(values)


def across(value, step):
    return lax.ppermute(value, ("xh", "xl"), [(i, i ^ step) for i in range(4)])


def ring_first(value):
    return shift(value, "x", 1), shift(value, "x", -1)


def ring_second(below, above):
    return shift(below[:64], "x", 1), shift(above[64:], "x", -1)


def fold_first(parts):
    far = parts[2].astype(BF)
    return shift(far[:64], "x", 1), shift(far[64:], "x", -1)


def fold_second(parts, low, high):
    after_me = jnp.concatenate([parts[1][:64] + low.astype(F32), parts[1][64:]]).astype(BF)
    before_me = jnp.concatenate([parts[3][:64], parts[3][64:] + high.astype(F32)]).astype(BF)
    return shift(after_me, "x", 1), shift(before_me, "x", -1)


def sum_parts(near, other):
    near, other = near.reshape(4, 128, D), other.reshape(4, 128, D)
    return [near[k].astype(F32) + other[k].astype(F32) for k in range(4)]


def exchange4(parts):
    xh, core = lax.axis_index("xh"), lax.axis_index("core")
    rel = [parts[0]]
    for turn in (1, 2, 3):
        rel.append(lax.ppermute(parts[turn], ("xh", "core"), [(i, i ^ turn) for i in range(4)]))
    me = 2 * xh + core
    rel = jnp.stack(rel)
    return jnp.concatenate([pick(rel, me ^ source) for source in range(4)])


def pair_gather(value, axis):
    me = lax.axis_index(axis)
    rel = jnp.stack([value, shift(value, axis, 1)])
    return jnp.where(me == 0, rel, rel[::-1])


def gather_plane(value):
    return lax.all_gather(value, PLANE, axis=0, tiled=False)


def scatter_plane_whole(value):
    flat = value.reshape(-1, value.shape[-1])
    return lax.psum_scatter(flat, PLANE, scatter_dimension=0, tiled=True)


STEPS = (("core", 1), ("y", 1), ("y", 2), ("z", 1), ("z", 2), ("xh", 1))


def toward(value, axis, bit):
    size = lax.axis_size(axis)
    return lax.ppermute(value, axis, [(i, i ^ bit) for i in range(size)])


def gather_step(value, step):
    axis, bit = STEPS[step]
    other = toward(value, axis, bit)
    high = (lax.axis_index(axis) & bit) != 0
    return jnp.concatenate([jnp.where(high, other, value), jnp.where(high, value, other)])


def reduce_step(value, step):
    axis, bit = STEPS[step]
    parts = value.reshape(2, value.shape[0] // 2, value.shape[1])
    mine = jnp.where((lax.axis_index(axis) & bit) != 0, 1, 0)
    return pick(parts, mine) + toward(pick(parts, 1 - mine), axis, bit)


def rehome(value, back=False, other=False):
    pairs = []
    for z in range(4):
        for y in range(4):
            for core in range(2):
                for xl in range(2):
                    owner = ((z * 4 + y) * 2 + core) * 2 + (xl ^ 1 if other else xl)
                    user = ((y * 4 + 2 * core + xl) * 2 + z // 2) * 2 + z % 2
                    pairs.append((user, owner) if back else (owner, user))
    return lax.ppermute(value, ("z", "y", "core", "xl"), pairs)


def owner_order(vector):
    lead = vector.shape[:-1]
    size = vector.shape[-1] // 32
    return jnp.swapaxes(vector.reshape(*lead, 2, 16, size), -3, -2).reshape(*lead, -1)


def plain_order(vector):
    lead = vector.shape[:-1]
    size = vector.shape[-1] // 32
    return jnp.swapaxes(vector.reshape(*lead, 16, 2, size), -3, -2).reshape(*lead, -1)


def dot(left, right):
    return jnp.dot(left, right, preferred_element_type=F32)


def dot_rows(left, right):
    return lax.dot_general(left, right, (((0,), (0,)), ((), ())), preferred_element_type=F32)


def dot_cols(left, right):
    return lax.dot_general(left, right, (((1,), (1,)), ((), ())), preferred_element_type=F32)


def deal_body(place_ref, up_ref, qkv_ref, proj_ref, down_ref, out_ref, proj_out, down_out):
    me, xl = place_ref[0], place_ref[1]
    proj_out[...] = proj_ref[pl.ds(pl.multiple_of(xl * 16, 16), 16), :]
    rows = pl.ds(pl.multiple_of(xl * 64, 64), 64)
    down_out[:64] = down_ref[rows, :1024]
    down_out[64:] = down_ref[rows, 1024:]
    lane = lax.broadcasted_iota(jnp.int32, (32, 128), 1)
    for turn in range(4):
        target = me ^ turn
        xh, core = lax.div(target, 2), lax.rem(target, 2)
        for pair in range(8):
            start = xh * 4096 + core * 128 + pair * 512
            left = up_ref[:, pl.ds(pl.multiple_of(start, 128), 128)].astype(F32)
            right = up_ref[:, pl.ds(pl.multiple_of(start + 256, 128), 128)].astype(F32)
            left = jnp.where(xl == 0, left, pltpu.roll(left, 64, 1))
            right = jnp.where(xl == 0, pltpu.roll(right, 64, 1), right)
            both = jnp.where(lane < 64, left, right).astype(BF)
            out_ref[turn, :, pair * 128 : (pair + 1) * 128] = both
        for block in range(3):
            start = block * D + xh * 1024 + core * 512 + xl * 256
            out_ref[turn, :, 1024 + block * 256 : 1280 + block * 256] = qkv_ref[
                :, pl.ds(pl.multiple_of(start, 256), 256)
            ]


def deal(me, xl, up, qkv, proj, down):
    vmem = pl.BlockSpec(memory_space=pltpu.VMEM)
    return pl.pallas_call(
        deal_body,
        in_specs=[pl.BlockSpec(memory_space=pltpu.SMEM), vmem, vmem, vmem, vmem],
        out_specs=[vmem] * 3,
        out_shape=[
            jax.ShapeDtypeStruct((4, 32, 1792), BF),
            jax.ShapeDtypeStruct((16, D), BF),
            jax.ShapeDtypeStruct((128, 1024), BF),
        ],
        name="deal",
    )(jnp.stack([me, xl]).astype(jnp.int32), up, qkv, proj, down)


def spread_body(place_ref, *refs):
    pieces, other_ref, down_own, proj_refs = refs[:4], refs[4], refs[5], refs[6:8]
    up_ref, qkv_ref, down_ref, proj_ref, held = refs[8:]
    place, core, xl = place_ref[0], place_ref[1], place_ref[2]
    for step in range(4):
        held[place ^ step, core] = pieces[step][:64]
        held[place ^ step, 1 - core] = other_ref[step]
    rows = pl.ds(pl.multiple_of(xl * 64, 64), 64)
    down_ref[rows, :1024] = down_own[:64].astype(F32)
    down_ref[rows, 1024:] = down_own[64:].astype(F32)
    rows = pl.ds(pl.multiple_of((1 - xl) * 64, 64), 64)
    down_ref[rows, :1024] = pieces[1][128:192].astype(F32)
    down_ref[rows, 1024:] = pieces[1][192:].astype(F32)
    for side in range(2):
        start = pl.multiple_of((xl ^ side) * 16, 16)
        proj_ref[pl.ds(start, 16), :] = proj_refs[side][...].astype(F32)
    for xh in range(2):
        for unit in range(16):
            for side in range(2):
                block = [
                    held[2 * xh + x, side, :32, unit * 64 : (unit + 1) * 64].astype(F32) for x in range(2)
                ]
                start = xh * 4096 + unit * 256 + side * 128
                up_ref[:, start : start + 128] = jnp.concatenate(block, axis=1)
        for side in range(2):
            for x in range(2):
                for block in range(3):
                    start = block * D + xh * 1024 + side * 512 + x * 256
                    qkv_ref[:, start : start + 256] = held[
                        2 * xh + x, side, 32:, block * 256 : (block + 1) * 256
                    ].astype(F32)


def spread(scalars, pieces, other, down, proj):
    vmem = pl.BlockSpec(memory_space=pltpu.VMEM)
    return pl.pallas_call(
        spread_body,
        in_specs=[pl.BlockSpec(memory_space=pltpu.SMEM)] + [vmem] * 8,
        out_specs=[vmem] * 4,
        out_shape=[
            jax.ShapeDtypeStruct((32, FF), F32),
            jax.ShapeDtypeStruct((32, 3 * D), F32),
            jax.ShapeDtypeStruct((128, D), F32),
            jax.ShapeDtypeStruct((32, D), F32),
        ],
        scratch_shapes=[pltpu.VMEM((4, 2, 64, 1024), BF)],
        name="spread",
    )(scalars, *pieces, other, down, *proj)


def merge_body(*refs):
    for step in range(4):
        refs[4][step] = refs[step][64:128]


def merge(pieces):
    vmem = pl.BlockSpec(memory_space=pltpu.VMEM)
    return pl.pallas_call(
        merge_body,
        in_specs=[vmem] * 4,
        out_specs=vmem,
        out_shape=jax.ShapeDtypeStruct((4, 64, 1024), BF),
        name="merge",
    )(*pieces)


def sort_body(place_ref, in_ref, *refs):
    down_ref, proj_ref = refs[4], refs[5]
    place, core = place_ref[0], place_ref[1]
    for step in range(4):
        xh = lax.div(place ^ step, 2)
        for side in range(2):
            start = pl.multiple_of(xh * 64 + (core ^ side) * 32, 32)
            at = side * 64
            refs[step][at : at + 32] = in_ref[pl.ds(start, 32), :]
            refs[step][at + 32 : at + 64] = in_ref[pl.ds(pl.multiple_of(start + 256, 32), 32), :]
    refs[1][128:] = in_ref[128:256, :]
    down_ref[...] = in_ref[128:256, :]
    for block in range(8):
        proj_ref[:, block * 256 : (block + 1) * 256] = in_ref[
            256 + block * 16 : 272 + block * 16, 768:
        ]


def sort(scalars, summed):
    vmem = pl.BlockSpec(memory_space=pltpu.VMEM)
    return pl.pallas_call(
        sort_body,
        in_specs=[pl.BlockSpec(memory_space=pltpu.SMEM), vmem],
        out_specs=[vmem] * 6,
        out_shape=[
            jax.ShapeDtypeStruct((256 if step == 1 else 128, 1024), BF) for step in range(4)
        ]
        + [jax.ShapeDtypeStruct((128, 1024), BF), jax.ShapeDtypeStruct((16, D), BF)],
        name="sort",
    )(scalars, summed)


def norm_body(near_ref, far_ref, gain_ref, shift_ref, normed_ref, turned_ref, mean_ref, rstd_ref):
    hidden = jnp.where(pl.program_id(0) < 2, near_ref[...], far_ref[...]).astype(F32)
    mean = jnp.mean(hidden, axis=-1, keepdims=True)
    centered = hidden - mean
    rstd = lax.rsqrt(jnp.mean(centered * centered, axis=-1, keepdims=True) + EPS)
    normed = (centered * rstd * gain_ref[...] + shift_ref[...]).astype(BF)
    normed_ref[...] = normed
    turned_ref[...] = normed.T
    mean_ref[...] = mean
    rstd_ref[...] = rstd


def norm(near, far, gain, shift_row):
    step = 256
    row = pl.BlockSpec((step, D), lambda i: (i, 0))
    vec = pl.BlockSpec((1, D), lambda i: (0, 0))
    one = pl.BlockSpec((step, 1), lambda i: (i, 0))
    return pl.pallas_call(
        norm_body,
        grid=(TOKENS // step,),
        in_specs=[
            pl.BlockSpec((step, D), lambda i: (jnp.minimum(i, 1), 0)),
            pl.BlockSpec((step, D), lambda i: (jnp.maximum(i - 2, 0), 0)),
            vec,
            vec,
        ],
        out_specs=[row, pl.BlockSpec((D, step), lambda i: (0, i)), one, one],
        out_shape=[
            jax.ShapeDtypeStruct((TOKENS, D), BF),
            jax.ShapeDtypeStruct((D, TOKENS), BF),
            jax.ShapeDtypeStruct((TOKENS, 1), F32),
            jax.ShapeDtypeStruct((TOKENS, 1), F32),
        ],
        compiler_params=pltpu.CompilerParams(vmem_limit_bytes=VMEM),
        cost_estimate=pl.CostEstimate(flops=20 << 20, bytes_accessed=12 << 20, transcendentals=0),
        name="norm",
    )(near, far, gain.reshape(1, D), shift_row.reshape(1, D))


def work_body(odd_ref, normed_hbm, turned_hbm, near_hbm, far_hbm, weights_hbm, bias_ref, up_bias_ref,
              cos_hbm, sin1_hbm, sin2_hbm, row_ref, col_hbm, ctx_hbm, out_hbm, act_hbm, grad_hbm, pack_hbm,
              cos_ref, sin1_ref, sin2_ref, col_ref, normed, turned, cot, ctx_ref, out_ref, weights, proj, merged, queries, keys, values, grads, mask, raw, pulled,
               probs, slopes, back_q, back_k, packed, sem, out_sems,
              up, down, act, units, upper_ref, slope_ref, up_out, down_out,
              act_sems, grad_sems, up_sems, down_sems):
    width = 4 * HD
    half = ROT // 2
    loads = [
        pltpu.make_async_copy(weights_hbm.at[:, pl.ds(256, 128), :], weights, sem.at[0]),
        pltpu.make_async_copy(normed_hbm.at[pl.ds(512, 512)], normed.at[pl.ds(512, 512)], sem.at[1]),
        pltpu.make_async_copy(near_hbm, cot.at[pl.ds(0, 512)], sem.at[2]),
        pltpu.make_async_copy(far_hbm, cot.at[pl.ds(512, 512)], sem.at[3]),
        pltpu.make_async_copy(turned_hbm, turned, sem.at[4]),
        pltpu.make_async_copy(cos_hbm, cos_ref, sem.at[5]),
        pltpu.make_async_copy(sin1_hbm, sin1_ref, sem.at[6]),
        pltpu.make_async_copy(sin2_hbm, sin2_ref, sem.at[7]),
        pltpu.make_async_copy(col_hbm, col_ref, sem.at[8]),
        pltpu.make_async_copy(normed_hbm.at[pl.ds(0, 512)], normed.at[pl.ds(0, 512)], sem.at[11]),
    ]
    up_load = pltpu.make_async_copy(weights_hbm.at[:, pl.ds(0, 128), :], up, sem.at[9])
    down_loads = [
        pltpu.make_async_copy(
            weights_hbm.at[:, pl.ds(128 + 64 * side, 64), :],
            down.at[:, :, pl.ds(1024 * side, 1024)],
            sem.at[(10, 12)[side]],
        )
        for side in range(2)
    ]
    for place in (0, 9):
        loads[place].start()
    odd = odd_ref[0]
    for k in range(2):
        probs[k, :128, 128:] = jnp.zeros((128, 128), BF)
        slopes[k, :128, 128:] = jnp.zeros((128, 128), BF)

    def sides(item):
        pair, base = lax.rem(item, 2), lax.div(item, 2) * 512
        first = pl.multiple_of(base + lax.rem(2 * pair + 3 * odd, 4) * 128, 128)
        second = pl.multiple_of(base + lax.rem(2 * pair + 3 * odd + 1, 4) * 128, 128)
        return first, second

    for place in (0, 9):
        loads[place].wait()
    for place in (5, 6, 7, 8, 1):
        loads[place].start()
    for block in range(8):
        proj[:, block * 256 : (block + 1) * 256] = weights[
            :, block * 16 : (block + 1) * 16, 768:
        ].reshape(256, 256)

    @pl.loop(0, 2)
    def _(step):
        @pl.when(step == 1)
        def _():
            loads[1].wait()
            loads[2].start()
            loads[3].start()

        rows = pl.ds(pl.multiple_of(step * 512, 512), 512)
        merged[...] = dot(normed[rows, :], weights[:, :, :768].reshape(D, 768)) + bias_ref[...]

        @pl.when(step == 0)
        def _():
            for place in (5, 6, 7, 8):
                loads[place].wait()

        @pl.loop(0, 4)
        def _(part):
            here = pl.ds(pl.multiple_of(part * 128, 128), 128)
            there = pl.ds(pl.multiple_of(step * 512 + part * 128, 128), 128)
            cosine, sin1, sin2 = cos_ref[there, :], sin1_ref[there, :], sin2_ref[there, :]
            for pair in range(2):
                for ref, base in ((queries, 0), (keys, width)):
                    value = merged[here, base + pair * 128 : base + (pair + 1) * 128]
                    value = (
                        value * cosine
                        - pltpu.roll(value, 128 - half, 1) * sin1
                        + pltpu.roll(value, half, 1) * sin2
                    )
                    ref[pair, there, :] = (value * SCALE if base == 0 else value).astype(BF)
                start = 2 * width + pair * 128
                values[pair, there, :] = merged[here, start : start + 128].astype(BF)

    loads[2].wait()
    loads[3].wait()
    up_load.start()
    loads[4].start()
    for load in down_loads:
        load.start()

    @pl.loop(0, 2)
    def _(step):
        rows = pl.ds(pl.multiple_of(step * 512, 512), 512)
        pulls = dot_cols(cot[rows, :], proj[...]).astype(BF)
        for pair in range(2):
            grads[pair, rows, :] = pulls[:, pair * 128 : (pair + 1) * 128]

    lane = lax.broadcasted_iota(jnp.int32, (SEQ, 128), 1)
    low = lane < HD

    @pl.loop(0, 4)
    def _(item):
        first, second = sides(item)
        segment = row_ref[item]
        for start in range(0, SEQ, 64):
            side = first if start < 128 else second
            rows = lax.broadcasted_iota(jnp.int32, (64, SEQ), 0) + start
            cols = lax.broadcasted_iota(jnp.int32, (64, SEQ), 1)
            own = col_ref[pl.ds(pl.multiple_of(side + start % 128, 64), 64), :]
            allowed = (cols <= rows) & (own == segment)
            mask[start : start + 64, :] = jnp.where(allowed, 0.0, -1e30)

        for pair in range(2):

            def load(ref):
                return jnp.concatenate([ref[pair, pl.ds(first, 128), :], ref[pair, pl.ds(second, 128), :]])

            query, key, value, grad = load(queries), load(keys), load(values), load(grads)
            for k in range(2):
                own = low if k == 0 else ~low
                raw[k] = dot_cols(jnp.where(own, query, 0), key)
                pulled[k] = dot_cols(jnp.where(own, grad, 0), value)
            for k in range(2):
                for start in range(0, SEQ, 32):
                    size = 128 if start < 128 else SEQ
                    rows = slice(start, start + 32)
                    scores = raw[k, rows, :size] + mask[rows, :size]
                    top = jnp.max(scores, axis=-1, keepdims=True)
                    expo = jnp.exp(scores - top)
                    prob = expo * (1.0 / jnp.sum(expo, axis=-1, keepdims=True))
                    probs[k, rows, :size] = prob.astype(BF)
                    grad_prob = pulled[k, rows, :size]
                    inner = jnp.sum(prob * grad_prob, axis=-1, keepdims=True)
                    slopes[k, rows, :size] = (prob * (grad_prob - inner)).astype(BF)
            context = jnp.where(low, dot(probs[0], value), dot(probs[1], value)).astype(BF)
            grad_v = jnp.where(low, dot_rows(probs[0], grad), dot_rows(probs[1], grad)).astype(BF)
            back_q[...] = SCALE * jnp.where(low, dot(slopes[0], key), dot(slopes[1], key))
            back_k[...] = jnp.where(low, dot_rows(slopes[0], query), dot_rows(slopes[1], query))
            lanes = slice(pair * 128, (pair + 1) * 128)
            for at, side in ((0, first), (128, second)):
                rows = pl.ds(side, 128)
                ctx_ref[rows, lanes] = context[at : at + 128]
                out_ref[rows, 2 * width + pair * 128 : 2 * width + (pair + 1) * 128] = grad_v[at : at + 128]
                for start in range(0, 128, 32):
                    there = pl.ds(pl.multiple_of(side + start, 32), 32)
                    cosine, sin1, sin2 = cos_ref[there, :], sin1_ref[there, :], sin2_ref[there, :]
                    for ref, base in ((back_q, 0), (back_k, width)):
                        turned_back = ref[at + start : at + start + 32, :]
                        turned_back = (
                            turned_back * cosine
                            + pltpu.roll(turned_back, 128 - half, 1) * sin1
                            - pltpu.roll(turned_back, half, 1) * sin2
                        )
                        out_ref[there, base + pair * 128 : base + (pair + 1) * 128] = turned_back.astype(BF)

    def store(step):
        owners = pl.ds(step * 4, 4)
        return pltpu.make_async_copy(
            packed.at[owners], pack_hbm.at[owners, pl.ds(256, 128), :], out_sems.at[step]
        )

    ctx_store = pltpu.make_async_copy(ctx_ref, ctx_hbm, sem.at[0])
    out_store = pltpu.make_async_copy(out_ref, out_hbm, sem.at[1])
    ctx_store.start()
    out_store.start()

    total = dot_rows(ctx_ref[...], cot[...]).astype(BF)
    for block in range(8):
        packed[:, block * 16 : (block + 1) * 16, 768:] = total[
            :, block * 256 : (block + 1) * 256
        ].reshape(16, 16, 256)
    loads[4].wait()

    @pl.loop(0, 4)
    def _(step):
        rows = pl.ds(pl.multiple_of(step * 512, 512), 512)
        total = dot(turned[rows, :], out_ref[...]).astype(BF)
        packed[pl.ds(step * 4, 4), :, :768] = total.reshape(4, 128, 768)
        store(step).start()

    def act_store(step):
        rows = pl.ds(pl.multiple_of(step * 512, 512), 512)
        return pltpu.make_async_copy(act.at[rows, :], act_hbm.at[rows, :], act_sems.at[step])

    def grad_store(step):
        rows = pl.ds(pl.multiple_of(step * 512, 512), 512)
        return pltpu.make_async_copy(units.at[rows, :], grad_hbm.at[rows, :], grad_sems.at[step])

    def up_store(step):
        owners = pl.ds(step * 4, 4)
        return pltpu.make_async_copy(
            up_out.at[owners], pack_hbm.at[owners, pl.ds(0, 128), :], up_sems.at[step]
        )

    def down_store(step):
        owners = pl.ds(step * 4, 4)
        return pltpu.make_async_copy(
            down_out.at[owners], pack_hbm.at[owners, pl.ds(128, 128), :], down_sems.at[step]
        )

    root = math.sqrt(2.0 / math.pi)
    up_load.wait()

    @pl.loop(0, 2)
    def _(step):
        rows = pl.ds(pl.multiple_of(step * 512, 512), 512)
        upper_ref[rows, :] = dot(normed[rows, :], up[...].reshape(D, 1024)) + up_bias_ref[...]

    for load in down_loads:
        load.wait()

    @pl.loop(0, 2)
    def _(step):
        rows = pl.ds(pl.multiple_of(step * 512, 512), 512)
        slope_ref[...] = dot_cols(cot[rows, :], down[...].reshape(1024, D))

        @pl.loop(0, 32)
        def _(part):
            here = pl.ds(pl.multiple_of(part * 16, 16), 16)
            there = pl.ds(pl.multiple_of(step * 512 + part * 16, 16), 16)
            for side in range(2):
                lanes = slice(side * 512, side * 512 + 512)
                upper = upper_ref[there, lanes]
                square = upper * upper
                bend = jnp.tanh(upper * (root + (root * 0.044715) * square))
                half = 0.5 + 0.5 * bend
                slope = half + upper * (0.5 - 0.5 * (bend * bend)) * (root + (root * 3 * 0.044715) * square)
                act[there, lanes] = (upper * half).astype(BF)
                units[there, lanes] = (slope_ref[here, lanes] * slope).astype(BF)

        act_store(step).start()
        grad_store(step).start()

    @pl.loop(0, 4)
    def _(step):
        rows = pl.ds(pl.multiple_of(step * 512, 512), 512)
        total = dot(turned[rows, :], units[...]).astype(BF)
        up_out[pl.ds(step * 4, 4)] = total.reshape(4, 128, 1024)
        up_store(step).start()

    @pl.loop(0, 4)
    def _(step):
        lanes = pl.ds(pl.multiple_of(step * 256, 256), 256)
        total = dot_rows(act[:, lanes], cot[...]).astype(BF)
        down_out[pl.ds(step * 4, 4), :64] = total[:, :1024].reshape(4, 64, 1024)
        down_out[pl.ds(step * 4, 4), 64:] = total[:, 1024:].reshape(4, 64, 1024)
        down_store(step).start()

    for step in range(2):
        act_store(step).wait()
        grad_store(step).wait()

    @pl.loop(0, 4)
    def _(step):
        down_store(step).wait()

    @pl.loop(0, 4)
    def _(step):
        up_store(step).wait()

    ctx_store.wait()
    out_store.wait()

    @pl.loop(0, 4)
    def _(step):
        store(step).wait()


def work(odd, normed, turned, near, far, weights, bias, up_bias, cosine, sin1, sin2, segment):
    blocks = segment.reshape(2, 4, 128)
    rows = jnp.where(odd == 0, blocks, jnp.roll(blocks, 1, axis=1)).reshape(4, 1, SEQ)
    vmem, hbm = pl.BlockSpec(memory_space=pltpu.VMEM), pl.BlockSpec(memory_space=pltpu.HBM)
    table = pltpu.VMEM((TOKENS, 128), F32)
    head_b = pltpu.VMEM((2, TOKENS, 128), BF)
    head_f = pltpu.VMEM((SEQ, 128), F32)
    slab = pltpu.VMEM((16, 128, 1024), BF)
    square = pltpu.VMEM((TOKENS, 1024), BF)
    return pl.pallas_call(
        work_body,
        in_specs=[pl.BlockSpec(memory_space=pltpu.SMEM)]
        + [hbm] * 5
        + [vmem] * 2
        + [hbm] * 3
        + [vmem, hbm],
        out_specs=[hbm] * 5,
        out_shape=[
            jax.ShapeDtypeStruct((TOKENS, 4 * HD), BF),
            jax.ShapeDtypeStruct((TOKENS, 12 * HD), BF),
            jax.ShapeDtypeStruct((TOKENS, 1024), BF),
            jax.ShapeDtypeStruct((TOKENS, 1024), BF),
            jax.ShapeDtypeStruct((16, 384, 1024), BF),
        ],
        scratch_shapes=[
            table,
            table,
            table,
            pltpu.VMEM((TOKENS, 1), jnp.int32),
            pltpu.VMEM((TOKENS, D), BF),
            pltpu.VMEM((D, TOKENS), BF),
            pltpu.VMEM((TOKENS, D), BF),
            pltpu.VMEM((TOKENS, 4 * HD), BF),
            pltpu.VMEM((TOKENS, 12 * HD), BF),
            slab,
            pltpu.VMEM((256, D), BF),
            pltpu.VMEM((512, 12 * HD), F32),
            head_b,
            head_b,
            head_b,
            head_b,
            pltpu.VMEM((SEQ, SEQ), F32),
            pltpu.VMEM((2, SEQ, SEQ), F32),
            pltpu.VMEM((2, SEQ, SEQ), F32),
            pltpu.VMEM((2, SEQ, SEQ), BF),
            pltpu.VMEM((2, SEQ, SEQ), BF),
            head_f,
            head_f,
            slab,
            pltpu.SemaphoreType.DMA((13,)),
            pltpu.SemaphoreType.DMA((8,)),
            slab,
            pltpu.VMEM((16, 64, D), BF),
            square,
            square,
            pltpu.VMEM((TOKENS, 1024), F32),
            pltpu.VMEM((512, 1024), F32),
            slab,
            slab,
            pltpu.SemaphoreType.DMA((4,)),
            pltpu.SemaphoreType.DMA((4,)),
            pltpu.SemaphoreType.DMA((8,)),
            pltpu.SemaphoreType.DMA((4,)),
        ],
        compiler_params=pltpu.CompilerParams(vmem_limit_bytes=VMEM),
        cost_estimate=pl.CostEstimate(
            flops=30 << 30, bytes_accessed=64 << 20, transcendentals=2 * TOKENS * 1024
        ),
        name="work",
    )(
        odd.reshape(1), normed, turned, near, far, weights, bias, up_bias, cosine, sin1, sin2, rows,
        segment.reshape(TOKENS, 1),
    )


def branch_body(context_ref, proj_ref, act_ref, down_ref, near_ref, far_ref):
    total = dot(act_ref[...], down_ref[...].reshape(1024, 256))
    total = (total + dot(context_ref[...], proj_ref[...].reshape(256, 256))).astype(BF)
    near_ref[...] = total[:512]
    far_ref[...] = total[512:]


def branch_out(context, active, weights):
    return pl.pallas_call(
        branch_body,
        grid=(8,),
        in_specs=[
            pl.BlockSpec((TOKENS, 256), lambda n: (0, 0), pipeline_mode=pl.Buffered(1)),
            pl.BlockSpec((16, 16, 256), lambda n: (0, 16 + n, 3)),
            pl.BlockSpec((TOKENS, 1024), lambda n: (0, 0), pipeline_mode=pl.Buffered(1)),
            pl.BlockSpec((16, 64, 256), lambda n: (0, 2 + n // 4, n % 4)),
        ],
        out_specs=[pl.BlockSpec((512, 256), lambda n: (0, n))] * 2,
        out_shape=[jax.ShapeDtypeStruct((512, D), BF)] * 2,
        compiler_params=pltpu.CompilerParams(vmem_limit_bytes=VMEM),
        cost_estimate=pl.CostEstimate(
            flops=2 * TOKENS * D * 1280, bytes_accessed=12 << 20, transcendentals=0
        ),
        name="branch",
    )(context, weights, active, weights)


def pull_body(grad_ref, merged_ref, up_ref, qkv_ref, hid_near_ref, hid_far_ref, mean_ref, rstd_ref,
              near_ref, far_ref, gain_ref, shift_ref, up_ref_sum, qkv_ref_sum):
    total = dot_cols(grad_ref[...], up_ref[...].reshape(256, 1024))
    total = total + dot_cols(merged_ref[...], qkv_ref[...].reshape(256, 1024)[:, :768])
    near_ref[...] = total[:512].astype(BF)
    far_ref[...] = total[512:].astype(BF)
    hidden = jnp.concatenate([hid_near_ref[...], hid_far_ref[...]]).astype(F32)
    normal = (hidden - mean_ref[...]) * rstd_ref[...]
    gain_ref[...] = jnp.sum(total * normal, axis=0, keepdims=True)
    shift_ref[...] = jnp.sum(total, axis=0, keepdims=True)

    @pl.when(pl.program_id(0) == 0)
    def _():
        ones = jnp.ones((16, TOKENS), BF)
        up_ref_sum[...] = dot(ones, grad_ref[...])[:1]
        qkv_ref_sum[...] = dot(ones, merged_ref[...])[:1]


def pull(grad_upper, grad_merged, weights, near, far, mean, rstd):
    def whole(width):
        return pl.BlockSpec((TOKENS, width), lambda n: (0, 0), pipeline_mode=pl.Buffered(1))

    half = pl.BlockSpec((512, 256), lambda n: (0, n))
    vec = pl.BlockSpec((1, 256), lambda n: (0, n))
    return pl.pallas_call(
        pull_body,
        grid=(8,),
        in_specs=[
            whole(1024),
            whole(768),
            pl.BlockSpec((2, 128, 1024), lambda n: (n, 0, 0)),
            pl.BlockSpec((2, 128, 1024), lambda n: (n, 2, 0)),
            half,
            half,
            whole(1),
            whole(1),
        ],
        out_specs=[half] * 2
        + [vec, vec, pl.BlockSpec((1, 1024), lambda n: (0, 0)), pl.BlockSpec((1, 768), lambda n: (0, 0))],
        out_shape=[
            jax.ShapeDtypeStruct((512, D), BF),
            jax.ShapeDtypeStruct((512, D), BF),
            jax.ShapeDtypeStruct((1, D), F32),
            jax.ShapeDtypeStruct((1, D), F32),
            jax.ShapeDtypeStruct((1, 1024), F32),
            jax.ShapeDtypeStruct((1, 768), F32),
        ],
        compiler_params=pltpu.CompilerParams(vmem_limit_bytes=VMEM),
        cost_estimate=pl.CostEstimate(
            flops=2 * TOKENS * D * 1792, bytes_accessed=16 << 20, transcendentals=0
        ),
        name="pull",
    )(grad_upper, grad_merged, weights, weights, near, far, mean, rstd)


def local(
    hidden_in, norm_gain, norm_shift, qkv_weight, qkv_bias, proj_weight, proj_bias,
    up_weight, up_bias, down_weight, down_bias, segment_ids, positions, cotangent,
):
    xh, core, xl = lax.axis_index("xh"), lax.axis_index("core"), lax.axis_index("xl")
    place = 2 * xh + xl
    scalars = jnp.stack([place, core, xl]).astype(jnp.int32)
    hidden_own = hidden_in.reshape(128, D)
    cot_own = cotangent.reshape(128, D)

    parts, proj_part, down_part = deal(
        2 * xh + core, xl, up_weight, qkv_weight, proj_weight, down_weight
    )
    parts = exchange4(parts)
    proj_part = rehome(proj_part)
    proj_part = proj_part.reshape(16, 8, 256).swapaxes(0, 1).reshape(128, 256)
    send = jnp.concatenate(
        [
            parts[:, :1024],
            down_part,
            jnp.concatenate([parts[:, 1024:], proj_part], axis=1),
        ]
    )

    small = jnp.concatenate([norm_gain, norm_shift, proj_bias, down_bias, qkv_bias, up_bias])[None]
    hidden_turned = owner_order(hidden_own)
    marks = jnp.stack(
        [positions.reshape(128), lax.dynamic_slice_in_dim(segment_ids.reshape(SEQ), xl * 128, 128)]
    )
    small, hidden_turned, cot_sent, marks, send = tie(small, hidden_turned, cot_own, marks, send)
    weights = gather_plane(send)
    small = gather_step(gather_step(small, 0), 1)
    small, hidden_turned = tie(small, hidden_turned)
    hid_below, hid_above = ring_first(hidden_turned)
    small = gather_step(small, 2)
    small, hid_below, hid_above = tie(small, hid_below, hid_above)
    hid_low, hid_high = ring_second(hid_below, hid_above)
    small, hid_low, hid_high, cot_sent = tie(small, hid_low, hid_high, cot_sent)
    hid = jnp.concatenate([hidden_turned, hid_above, hid_low, hid_high, hid_below])
    hid_far = shift(hid, "core", 1)
    cot_below, cot_above = ring_first(cot_sent)
    small = gather_step(small, 3)
    small, marks, cot_below, cot_above = tie(small, marks, cot_below, cot_above)
    cot_low, cot_high = ring_second(cot_below, cot_above)
    small = gather_step(small, 4)
    small, marks, cot_low, cot_high = tie(small, marks, cot_low, cot_high)
    cot = jnp.concatenate([cot_sent, cot_above, cot_low, cot_high, cot_below])
    cot_far = shift(cot, "core", 1)
    marks = pair_gather(marks, "xl")
    small = gather_step(small, 5).astype(F32)
    marks = pair_gather(marks, "xh").reshape(4, 2, 128)
    marks = jnp.stack([pick(marks, (place + k) % 4) for k in range(4)])
    marks = jnp.stack([marks, shift(marks, "core", 1)]).transpose(2, 0, 1, 3).reshape(2, TOKENS)
    position_all, segment_all = marks[0], marks[1]

    gain = owner_order(small[:, :32].reshape(D))
    shift_row = owner_order(small[:, 32:64].reshape(D))
    out_bias = (small[:, 64:96] + small[:, 96:128]).reshape(D)
    qkv_b = small[:, 128:224].reshape(3, 2, 2, 2, 256)[:, xh, core, xl].reshape(1, 768)
    up_b = small[:, 224:352].reshape(2, 16, 2, 128)[xh, :, core]
    up_b = lax.dynamic_slice_in_dim(up_b, xl * 64, 64, 1).reshape(1, 1024)
    normed, turned, mean, rstd = norm(hid, hid_far, gain, shift_row)

    lane = jnp.arange(128) % HD
    freqs = 10000.0 ** (-(lane % 16).astype(F32) * (2.0 / ROT))
    angles = position_all.astype(F32)[:, None] * freqs
    cosine = jnp.where(lane < ROT, jnp.cos(angles), 1.0)
    sine = jnp.sin(angles)
    sin1 = jnp.where(lane < 16, sine, 0.0)
    sin2 = jnp.where((lane >= 16) & (lane < ROT), sine, 0.0)

    context, grad_merged, active, grad_upper, pack = work(
        xl, normed, turned, cot, cot_far, weights, qkv_b, up_b, cosine, sin1, sin2, segment_all
    )
    back = scatter_plane_whole(pack)

    pulled, pulled_far, gain_sum, shift_sum, up_sum, qkv_sum = pull(
        grad_upper, grad_merged, weights, hid, hid_far, mean, rstd
    )
    out_sum = jnp.sum(cot_own.astype(F32), axis=0)
    qkv_full = lax.dynamic_update_slice(
        jnp.zeros((3, 2, 2, 2, 256), F32), qkv_sum.reshape(3, 1, 1, 1, 256), (0, xh, core, xl, 0)
    )
    up_full = lax.dynamic_update_slice(
        jnp.zeros((2, 16, 2, 2, 64), F32), up_sum.reshape(1, 16, 1, 1, 64), (xh, 0, core, xl, 0)
    )
    sums = jnp.concatenate(
        [plain_order(s.reshape(D)).reshape(64, 32) for s in (gain_sum, shift_sum)]
        + [out_sum.reshape(64, 32), qkv_full.reshape(64, 96), up_full.reshape(64, 128)],
        axis=1,
    )
    pulled_far = shift(pulled_far, "core", 1)
    sums = reduce_step(sums, 5)
    branch, branch_far = branch_out(context, active, weights)
    sums, branch_far, pulled_far = tie(sums, branch_far, pulled_far)
    pulled = sum_parts(pulled, pulled_far)
    low, high = fold_first(pulled)
    branch_far = shift(branch_far, "core", 1)
    sums = reduce_step(reduce_step(reduce_step(sums, 4), 3), 2)
    sums, branch_far, low, high = tie(sums, branch_far, low, high)
    from_below, from_above = fold_second(pulled, low, high)
    branch = sum_parts(branch, branch_far)
    low, high = fold_first(branch)
    sums = reduce_step(reduce_step(sums, 1), 0)
    sums = (sums + shift(sums, "xl", 1))[0]
    sums, low, high, from_below, from_above = tie(sums, low, high, from_below, from_above)
    branch_below, branch_above = fold_second(branch, low, high)
    grad_own = pulled[0] + from_below.astype(F32) + from_above.astype(F32)

    own = owner_order(hidden_own).astype(F32)
    mean = jnp.mean(own, axis=-1, keepdims=True)
    centered = own - mean
    rstd = lax.rsqrt(jnp.mean(centered * centered, axis=-1, keepdims=True) + EPS)
    normal_own = centered * rstd
    scaled = grad_own * gain
    inner = jnp.mean(scaled * normal_own, axis=-1, keepdims=True)
    lifted = (scaled - jnp.mean(scaled, axis=-1, keepdims=True) - normal_own * inner) * rstd
    grad_hidden = (cot_own.astype(F32) + plain_order(lifted)).reshape(1, 128, D)

    branch = branch[0] + branch_below.astype(F32) + branch_above.astype(F32)
    block_out = hidden_own.astype(F32) + branch + out_bias
    block_out = block_out.astype(BF).reshape(1, 128, D)

    back, grad_hidden, block_out, sums = tie(back, grad_hidden, block_out, sums)
    *pieces, down_rows, proj_rows = sort(scalars, back)
    pieces = [pieces[0]] + [across(pieces[step], step) for step in (1, 2, 3)]
    proj = (rehome(proj_rows, back=True), rehome(proj_rows, back=True, other=True))
    pieces, proj = tie(pieces, proj)
    other = shift(merge(pieces), "core", 1)
    grad_up, grad_qkv, grad_down, grad_proj = spread(scalars, pieces, other, down_rows, proj)
    return (
        block_out,
        grad_hidden,
        sums[:32],
        sums[32:64],
        grad_qkv,
        sums[96:192],
        grad_proj,
        sums[64:96],
        grad_up,
        sums[192:320],
        grad_down,
        sums[64:96],
    )


def solution(mesh):
    cut = Mesh(mesh.devices.reshape(2, 4, 4, 2, 2), AXES)
    row, vec = P(SHARD, None), P(SHARD)
    tok = P(SHARD, "xl", None)
    return jax.shard_map(
        local,
        mesh=cut,
        in_specs=(
            tok, vec, vec, row, vec, row, vec, row, vec, row, vec, row, P(SHARD, "xl"), tok,
        ),
        out_specs=(tok, tok, vec, vec, row, vec, row, vec, row, vec, row, vec),
        check_vma=False,
    )
```

```python
import math

import jax
import jax.numpy as jnp
from jax import lax
from jax.experimental import pallas as pl
from jax.experimental.pallas import tpu as pltpu
from jax.sharding import Mesh, PartitionSpec as P

D = 2048
H = 32
HD = 64
ROT = 32
FF = 8192
SEQ = 256
SCALE = HD**-0.5
EPS = 1e-5
VMEM = 60 << 20
AXES = ("xh", "z", "y", "core", "xl")
SHARD = ("xh", "z", "y", "core")
PLANE = ("z", "y")
TOKENS = 1024
BF = jnp.bfloat16
F32 = jnp.float32


def shift(value, axis, step):
    names, size = (("xh", "xl"), 4) if axis == "x" else (axis, lax.axis_size(axis))
    return lax.ppermute(value, names, [(i, (i + step) % size) for i in range(size)])


def pick(value, index, axis=0):
    return lax.dynamic_index_in_dim(value, index, axis, keepdims=False)


def tie(*values):
    return lax.optimization_barrier(values)


def across(value, step):
    return lax.ppermute(value, ("xh", "xl"), [(i, i ^ step) for i in range(4)])


def ring_first(value):
    return shift(value, "x", 1), shift(value, "x", -1)


def ring_second(below, above):
    return shift(below[:64], "x", 1), shift(above[64:], "x", -1)


def fold_first(parts):
    far = parts[2].astype(BF)
    return shift(far[:64], "x", 1), shift(far[64:], "x", -1)


def fold_second(parts, low, high):
    after_me = jnp.concatenate([parts[1][:64] + low.astype(F32), parts[1][64:]]).astype(BF)
    before_me = jnp.concatenate([parts[3][:64], parts[3][64:] + high.astype(F32)]).astype(BF)
    return shift(after_me, "x", 1), shift(before_me, "x", -1)


def sum_parts(near, other):
    near, other = near.reshape(4, 128, D), other.reshape(4, 128, D)
    return [near[k].astype(F32) + other[k].astype(F32) for k in range(4)]


def exchange4(parts):
    xh, core = lax.axis_index("xh"), lax.axis_index("core")
    rel = [parts[0]]
    for turn in (1, 2, 3):
        rel.append(lax.ppermute(parts[turn], ("xh", "core"), [(i, i ^ turn) for i in range(4)]))
    me = 2 * xh + core
    rel = jnp.stack(rel)
    return jnp.concatenate([pick(rel, me ^ source) for source in range(4)])


def pair_gather(value, axis):
    me = lax.axis_index(axis)
    rel = jnp.stack([value, shift(value, axis, 1)])
    return jnp.where(me == 0, rel, rel[::-1])


def gather_plane(value):
    return lax.all_gather(value, PLANE, axis=0, tiled=False)


def scatter_plane_whole(value):
    flat = value.reshape(-1, value.shape[-1])
    return lax.psum_scatter(flat, PLANE, scatter_dimension=0, tiled=True)


STEPS = (("core", 1), ("y", 1), ("y", 2), ("z", 1), ("z", 2), ("xh", 1))


def toward(value, axis, bit):
    size = lax.axis_size(axis)
    return lax.ppermute(value, axis, [(i, i ^ bit) for i in range(size)])


def gather_step(value, step):
    axis, bit = STEPS[step]
    other = toward(value, axis, bit)
    high = (lax.axis_index(axis) & bit) != 0
    return jnp.concatenate([jnp.where(high, other, value), jnp.where(high, value, other)])


def reduce_step(value, step):
    axis, bit = STEPS[step]
    parts = value.reshape(2, value.shape[0] // 2, value.shape[1])
    mine = jnp.where((lax.axis_index(axis) & bit) != 0, 1, 0)
    return pick(parts, mine) + toward(pick(parts, 1 - mine), axis, bit)


def rehome(value, back=False, other=False):
    pairs = []
    for z in range(4):
        for y in range(4):
            for core in range(2):
                for xl in range(2):
                    owner = ((z * 4 + y) * 2 + core) * 2 + (xl ^ 1 if other else xl)
                    user = ((y * 4 + 2 * core + xl) * 2 + z // 2) * 2 + z % 2
                    pairs.append((user, owner) if back else (owner, user))
    return lax.ppermute(value, ("z", "y", "core", "xl"), pairs)


def owner_order(vector):
    lead = vector.shape[:-1]
    size = vector.shape[-1] // 32
    return jnp.swapaxes(vector.reshape(*lead, 2, 16, size), -3, -2).reshape(*lead, -1)


def plain_order(vector):
    lead = vector.shape[:-1]
    size = vector.shape[-1] // 32
    return jnp.swapaxes(vector.reshape(*lead, 16, 2, size), -3, -2).reshape(*lead, -1)


def dot(left, right):
    return jnp.dot(left, right, preferred_element_type=F32)


def dot_rows(left, right):
    return lax.dot_general(left, right, (((0,), (0,)), ((), ())), preferred_element_type=F32)


def dot_cols(left, right):
    return lax.dot_general(left, right, (((1,), (1,)), ((), ())), preferred_element_type=F32)


def deal_body(place_ref, up_ref, qkv_ref, proj_ref, down_ref, out_ref, proj_out, down_out):
    me, xl = place_ref[0], place_ref[1]
    proj_out[...] = proj_ref[pl.ds(pl.multiple_of(xl * 16, 16), 16), :]
    rows = pl.ds(pl.multiple_of(xl * 64, 64), 64)
    down_out[:64] = down_ref[rows, :1024]
    down_out[64:] = down_ref[rows, 1024:]
    lane = lax.broadcasted_iota(jnp.int32, (32, 128), 1)
    for turn in range(4):
        target = me ^ turn
        xh, core = lax.div(target, 2), lax.rem(target, 2)
        for pair in range(8):
            start = xh * 4096 + core * 128 + pair * 512
            left = up_ref[:, pl.ds(pl.multiple_of(start, 128), 128)].astype(F32)
            right = up_ref[:, pl.ds(pl.multiple_of(start + 256, 128), 128)].astype(F32)
            left = jnp.where(xl == 0, left, pltpu.roll(left, 64, 1))
            right = jnp.where(xl == 0, pltpu.roll(right, 64, 1), right)
            both = jnp.where(lane < 64, left, right).astype(BF)
            out_ref[turn, :, pair * 128 : (pair + 1) * 128] = both
        for block in range(3):
            start = block * D + xh * 1024 + core * 512 + xl * 256
            out_ref[turn, :, 1024 + block * 256 : 1280 + block * 256] = qkv_ref[
                :, pl.ds(pl.multiple_of(start, 256), 256)
            ]


def deal(me, xl, up, qkv, proj, down):
    vmem = pl.BlockSpec(memory_space=pltpu.VMEM)
    return pl.pallas_call(
        deal_body,
        in_specs=[pl.BlockSpec(memory_space=pltpu.SMEM), vmem, vmem, vmem, vmem],
        out_specs=[vmem] * 3,
        out_shape=[
            jax.ShapeDtypeStruct((4, 32, 1792), BF),
            jax.ShapeDtypeStruct((16, D), BF),
            jax.ShapeDtypeStruct((128, 1024), BF),
        ],
        name="deal",
    )(jnp.stack([me, xl]).astype(jnp.int32), up, qkv, proj, down)


def spread_body(place_ref, *refs):
    pieces, other_ref, down_own, proj_refs = refs[:4], refs[4], refs[5], refs[6:8]
    up_ref, qkv_ref, down_ref, proj_ref, held = refs[8:]
    place, core, xl = place_ref[0], place_ref[1], place_ref[2]
    for step in range(4):
        held[place ^ step, core] = pieces[step][:64]
        held[place ^ step, 1 - core] = other_ref[step]
    rows = pl.ds(pl.multiple_of(xl * 64, 64), 64)
    down_ref[rows, :1024] = down_own[:64].astype(F32)
    down_ref[rows, 1024:] = down_own[64:].astype(F32)
    rows = pl.ds(pl.multiple_of((1 - xl) * 64, 64), 64)
    down_ref[rows, :1024] = pieces[1][128:192].astype(F32)
    down_ref[rows, 1024:] = pieces[1][192:].astype(F32)
    for side in range(2):
        start = pl.multiple_of((xl ^ side) * 16, 16)
        proj_ref[pl.ds(start, 16), :] = proj_refs[side][...].astype(F32)
    for xh in range(2):
        for unit in range(16):
            for side in range(2):
                block = [
                    held[2 * xh + x, side, :32, unit * 64 : (unit + 1) * 64].astype(F32) for x in range(2)
                ]
                start = xh * 4096 + unit * 256 + side * 128
                up_ref[:, start : start + 128] = jnp.concatenate(block, axis=1)
        for side in range(2):
            for x in range(2):
                for block in range(3):
                    start = block * D + xh * 1024 + side * 512 + x * 256
                    qkv_ref[:, start : start + 256] = held[
                        2 * xh + x, side, 32:, block * 256 : (block + 1) * 256
                    ].astype(F32)


def spread(scalars, pieces, other, down, proj):
    vmem = pl.BlockSpec(memory_space=pltpu.VMEM)
    return pl.pallas_call(
        spread_body,
        in_specs=[pl.BlockSpec(memory_space=pltpu.SMEM)] + [vmem] * 8,
        out_specs=[vmem] * 4,
        out_shape=[
            jax.ShapeDtypeStruct((32, FF), F32),
            jax.ShapeDtypeStruct((32, 3 * D), F32),
            jax.ShapeDtypeStruct((128, D), F32),
            jax.ShapeDtypeStruct((32, D), F32),
        ],
        scratch_shapes=[pltpu.VMEM((4, 2, 64, 1024), BF)],
        name="spread",
    )(scalars, *pieces, other, down, *proj)


def merge_body(*refs):
    for step in range(4):
        refs[4][step] = refs[step][64:128]


def merge(pieces):
    vmem = pl.BlockSpec(memory_space=pltpu.VMEM)
    return pl.pallas_call(
        merge_body,
        in_specs=[vmem] * 4,
        out_specs=vmem,
        out_shape=jax.ShapeDtypeStruct((4, 64, 1024), BF),
        name="merge",
    )(*pieces)


def sort_body(place_ref, in_ref, *refs):
    down_ref, proj_ref = refs[4], refs[5]
    place, core = place_ref[0], place_ref[1]
    for step in range(4):
        xh = lax.div(place ^ step, 2)
        for side in range(2):
            start = pl.multiple_of(xh * 64 + (core ^ side) * 32, 32)
            at = side * 64
            refs[step][at : at + 32] = in_ref[pl.ds(start, 32), :]
            refs[step][at + 32 : at + 64] = in_ref[pl.ds(pl.multiple_of(start + 256, 32), 32), :]
    refs[1][128:] = in_ref[128:256, :]
    down_ref[...] = in_ref[128:256, :]
    for block in range(8):
        proj_ref[:, block * 256 : (block + 1) * 256] = in_ref[
            256 + block * 16 : 272 + block * 16, 768:
        ]


def sort(scalars, summed):
    vmem = pl.BlockSpec(memory_space=pltpu.VMEM)
    return pl.pallas_call(
        sort_body,
        in_specs=[pl.BlockSpec(memory_space=pltpu.SMEM), vmem],
        out_specs=[vmem] * 6,
        out_shape=[
            jax.ShapeDtypeStruct((256 if step == 1 else 128, 1024), BF) for step in range(4)
        ]
        + [jax.ShapeDtypeStruct((128, 1024), BF), jax.ShapeDtypeStruct((16, D), BF)],
        name="sort",
    )(scalars, summed)


def norm_body(near_ref, far_ref, gain_ref, shift_ref, normed_ref, turned_ref, mean_ref, rstd_ref):
    hidden = jnp.where(pl.program_id(0) < 2, near_ref[...], far_ref[...]).astype(F32)
    mean = jnp.mean(hidden, axis=-1, keepdims=True)
    centered = hidden - mean
    rstd = lax.rsqrt(jnp.mean(centered * centered, axis=-1, keepdims=True) + EPS)
    normed = (centered * rstd * gain_ref[...] + shift_ref[...]).astype(BF)
    normed_ref[...] = normed
    turned_ref[...] = normed.T
    mean_ref[...] = mean
    rstd_ref[...] = rstd


def norm(near, far, gain, shift_row):
    step = 256
    row = pl.BlockSpec((step, D), lambda i: (i, 0))
    vec = pl.BlockSpec((1, D), lambda i: (0, 0))
    one = pl.BlockSpec((step, 1), lambda i: (i, 0))
    return pl.pallas_call(
        norm_body,
        grid=(TOKENS // step,),
        in_specs=[
            pl.BlockSpec((step, D), lambda i: (jnp.minimum(i, 1), 0)),
            pl.BlockSpec((step, D), lambda i: (jnp.maximum(i - 2, 0), 0)),
            vec,
            vec,
        ],
        out_specs=[row, pl.BlockSpec((D, step), lambda i: (0, i)), one, one],
        out_shape=[
            jax.ShapeDtypeStruct((TOKENS, D), BF),
            jax.ShapeDtypeStruct((D, TOKENS), BF),
            jax.ShapeDtypeStruct((TOKENS, 1), F32),
            jax.ShapeDtypeStruct((TOKENS, 1), F32),
        ],
        compiler_params=pltpu.CompilerParams(vmem_limit_bytes=VMEM),
        cost_estimate=pl.CostEstimate(flops=20 << 20, bytes_accessed=12 << 20, transcendentals=0),
        name="norm",
    )(near, far, gain.reshape(1, D), shift_row.reshape(1, D))


def work_body(odd_ref, normed_hbm, turned_hbm, near_hbm, far_hbm, weights_hbm, bias_ref, up_bias_ref,
              cos_hbm, sin1_hbm, sin2_hbm, row_ref, col_hbm, ctx_hbm, out_hbm, act_hbm, grad_hbm, pack_hbm,
              cos_ref, sin1_ref, sin2_ref, col_ref, normed, turned, cot, ctx_ref, out_ref, weights, proj, merged, queries, keys, values, grads, mask, raw, pulled,
               probs, slopes, back_q, back_k, packed, sem, out_sems,
              up, down, act, units, upper_ref, slope_ref, up_out, down_out,
              act_sems, grad_sems, up_sems, down_sems):
    width = 4 * HD
    half = ROT // 2
    loads = [
        pltpu.make_async_copy(weights_hbm.at[:, pl.ds(256, 128), :], weights, sem.at[0]),
        pltpu.make_async_copy(normed_hbm.at[pl.ds(512, 512)], normed.at[pl.ds(512, 512)], sem.at[1]),
        pltpu.make_async_copy(near_hbm, cot.at[pl.ds(0, 512)], sem.at[2]),
        pltpu.make_async_copy(far_hbm, cot.at[pl.ds(512, 512)], sem.at[3]),
        pltpu.make_async_copy(turned_hbm, turned, sem.at[4]),
        pltpu.make_async_copy(cos_hbm, cos_ref, sem.at[5]),
        pltpu.make_async_copy(sin1_hbm, sin1_ref, sem.at[6]),
        pltpu.make_async_copy(sin2_hbm, sin2_ref, sem.at[7]),
        pltpu.make_async_copy(col_hbm, col_ref, sem.at[8]),
        pltpu.make_async_copy(normed_hbm.at[pl.ds(0, 512)], normed.at[pl.ds(0, 512)], sem.at[11]),
    ]
    up_load = pltpu.make_async_copy(weights_hbm.at[:, pl.ds(0, 128), :], up, sem.at[9])
    down_loads = [
        pltpu.make_async_copy(
            weights_hbm.at[:, pl.ds(128 + 64 * side, 64), :],
            down.at[:, :, pl.ds(1024 * side, 1024)],
            sem.at[(10, 12)[side]],
        )
        for side in range(2)
    ]
    for place in (0, 9):
        loads[place].start()
    odd = odd_ref[0]
    for k in range(2):
        probs[k, :128, 128:] = jnp.zeros((128, 128), BF)
        slopes[k, :128, 128:] = jnp.zeros((128, 128), BF)

    def sides(item):
        pair, base = lax.rem(item, 2), lax.div(item, 2) * 512
        first = pl.multiple_of(base + lax.rem(2 * pair + 3 * odd, 4) * 128, 128)
        second = pl.multiple_of(base + lax.rem(2 * pair + 3 * odd + 1, 4) * 128, 128)
        return first, second

    for place in (0, 9):
        loads[place].wait()
    for place in (5, 6, 7, 8, 1):
        loads[place].start()
    for block in range(8):
        proj[:, block * 256 : (block + 1) * 256] = weights[
            :, block * 16 : (block + 1) * 16, 768:
        ].reshape(256, 256)

    @pl.loop(0, 2)
    def _(step):
        @pl.when(step == 1)
        def _():
            loads[1].wait()
            loads[2].start()
            loads[3].start()

        rows = pl.ds(pl.multiple_of(step * 512, 512), 512)
        merged[...] = dot(normed[rows, :], weights[:, :, :768].reshape(D, 768)) + bias_ref[...]

        @pl.when(step == 0)
        def _():
            for place in (5, 6, 7, 8):
                loads[place].wait()

        @pl.loop(0, 4)
        def _(part):
            here = pl.ds(pl.multiple_of(part * 128, 128), 128)
            there = pl.ds(pl.multiple_of(step * 512 + part * 128, 128), 128)
            cosine, sin1, sin2 = cos_ref[there, :], sin1_ref[there, :], sin2_ref[there, :]
            for pair in range(2):
                for ref, base in ((queries, 0), (keys, width)):
                    value = merged[here, base + pair * 128 : base + (pair + 1) * 128]
                    value = (
                        value * cosine
                        - pltpu.roll(value, 128 - half, 1) * sin1
                        + pltpu.roll(value, half, 1) * sin2
                    )
                    ref[pair, there, :] = (value * SCALE if base == 0 else value).astype(BF)
                start = 2 * width + pair * 128
                values[pair, there, :] = merged[here, start : start + 128].astype(BF)

    loads[2].wait()
    loads[3].wait()
    up_load.start()
    loads[4].start()
    for load in down_loads:
        load.start()

    @pl.loop(0, 2)
    def _(step):
        rows = pl.ds(pl.multiple_of(step * 512, 512), 512)
        pulls = dot_cols(cot[rows, :], proj[...]).astype(BF)
        for pair in range(2):
            grads[pair, rows, :] = pulls[:, pair * 128 : (pair + 1) * 128]

    lane = lax.broadcasted_iota(jnp.int32, (SEQ, 128), 1)
    low = lane < HD

    @pl.loop(0, 4)
    def _(item):
        first, second = sides(item)
        segment = row_ref[item]
        for start in range(0, SEQ, 64):
            side = first if start < 128 else second
            rows = lax.broadcasted_iota(jnp.int32, (64, SEQ), 0) + start
            cols = lax.broadcasted_iota(jnp.int32, (64, SEQ), 1)
            own = col_ref[pl.ds(pl.multiple_of(side + start % 128, 64), 64), :]
            allowed = (cols <= rows) & (own == segment)
            mask[start : start + 64, :] = jnp.where(allowed, 0.0, -1e30)

        for pair in range(2):

            def load(ref):
                return jnp.concatenate([ref[pair, pl.ds(first, 128), :], ref[pair, pl.ds(second, 128), :]])

            query, key, value, grad = load(queries), load(keys), load(values), load(grads)
            for k in range(2):
                own = low if k == 0 else ~low
                raw[k] = dot_cols(jnp.where(own, query, 0), key)
                pulled[k] = dot_cols(jnp.where(own, grad, 0), value)
            for k in range(2):
                for start in range(0, SEQ, 32):
                    size = 128 if start < 128 else SEQ
                    rows = slice(start, start + 32)
                    scores = raw[k, rows, :size] + mask[rows, :size]
                    top = jnp.max(scores, axis=-1, keepdims=True)
                    expo = jnp.exp(scores - top)
                    prob = expo * (1.0 / jnp.sum(expo, axis=-1, keepdims=True))
                    probs[k, rows, :size] = prob.astype(BF)
                    grad_prob = pulled[k, rows, :size]
                    inner = jnp.sum(prob * grad_prob, axis=-1, keepdims=True)
                    slopes[k, rows, :size] = (prob * (grad_prob - inner)).astype(BF)
            context = jnp.where(low, dot(probs[0], value), dot(probs[1], value)).astype(BF)
            grad_v = jnp.where(low, dot_rows(probs[0], grad), dot_rows(probs[1], grad)).astype(BF)
            back_q[...] = SCALE * jnp.where(low, dot(slopes[0], key), dot(slopes[1], key))
            back_k[...] = jnp.where(low, dot_rows(slopes[0], query), dot_rows(slopes[1], query))
            lanes = slice(pair * 128, (pair + 1) * 128)
            for at, side in ((0, first), (128, second)):
                rows = pl.ds(side, 128)
                ctx_ref[rows, lanes] = context[at : at + 128]
                out_ref[rows, 2 * width + pair * 128 : 2 * width + (pair + 1) * 128] = grad_v[at : at + 128]
                for start in range(0, 128, 32):
                    there = pl.ds(pl.multiple_of(side + start, 32), 32)
                    cosine, sin1, sin2 = cos_ref[there, :], sin1_ref[there, :], sin2_ref[there, :]
                    for ref, base in ((back_q, 0), (back_k, width)):
                        turned_back = ref[at + start : at + start + 32, :]
                        turned_back = (
                            turned_back * cosine
                            + pltpu.roll(turned_back, 128 - half, 1) * sin1
                            - pltpu.roll(turned_back, half, 1) * sin2
                        )
                        out_ref[there, base + pair * 128 : base + (pair + 1) * 128] = turned_back.astype(BF)

    def store(step):
        owners = pl.ds(step * 4, 4)
        return pltpu.make_async_copy(
            packed.at[owners], pack_hbm.at[owners, pl.ds(256, 128), :], out_sems.at[step]
        )

    ctx_store = pltpu.make_async_copy(ctx_ref, ctx_hbm, sem.at[0])
    out_store = pltpu.make_async_copy(out_ref, out_hbm, sem.at[1])
    ctx_store.start()
    out_store.start()

    total = dot_rows(ctx_ref[...], cot[...]).astype(BF)
    for block in range(8):
        packed[:, block * 16 : (block + 1) * 16, 768:] = total[
            :, block * 256 : (block + 1) * 256
        ].reshape(16, 16, 256)
    loads[4].wait()

    @pl.loop(0, 4)
    def _(step):
        rows = pl.ds(pl.multiple_of(step * 512, 512), 512)
        total = dot(turned[rows, :], out_ref[...]).astype(BF)
        packed[pl.ds(step * 4, 4), :, :768] = total.reshape(4, 128, 768)
        store(step).start()

    def act_store(step):
        rows = pl.ds(pl.multiple_of(step * 512, 512), 512)
        return pltpu.make_async_copy(act.at[rows, :], act_hbm.at[rows, :], act_sems.at[step])

    def grad_store(step):
        rows = pl.ds(pl.multiple_of(step * 512, 512), 512)
        return pltpu.make_async_copy(units.at[rows, :], grad_hbm.at[rows, :], grad_sems.at[step])

    def up_store(step):
        owners = pl.ds(step * 4, 4)
        return pltpu.make_async_copy(
            up_out.at[owners], pack_hbm.at[owners, pl.ds(0, 128), :], up_sems.at[step]
        )

    def down_store(step):
        owners = pl.ds(step * 4, 4)
        return pltpu.make_async_copy(
            down_out.at[owners], pack_hbm.at[owners, pl.ds(128, 128), :], down_sems.at[step]
        )

    root = math.sqrt(2.0 / math.pi)
    up_load.wait()

    @pl.loop(0, 2)
    def _(step):
        rows = pl.ds(pl.multiple_of(step * 512, 512), 512)
        upper_ref[rows, :] = dot(normed[rows, :], up[...].reshape(D, 1024)) + up_bias_ref[...]

    for load in down_loads:
        load.wait()

    @pl.loop(0, 2)
    def _(step):
        rows = pl.ds(pl.multiple_of(step * 512, 512), 512)
        slope_ref[...] = dot_cols(cot[rows, :], down[...].reshape(1024, D))

        @pl.loop(0, 32)
        def _(part):
            here = pl.ds(pl.multiple_of(part * 16, 16), 16)
            there = pl.ds(pl.multiple_of(step * 512 + part * 16, 16), 16)
            for side in range(2):
                lanes = slice(side * 512, side * 512 + 512)
                upper = upper_ref[there, lanes]
                square = upper * upper
                bend = jnp.tanh(upper * (root + (root * 0.044715) * square))
                half = 0.5 + 0.5 * bend
                slope = half + upper * (0.5 - 0.5 * (bend * bend)) * (root + (root * 3 * 0.044715) * square)
                act[there, lanes] = (upper * half).astype(BF)
                units[there, lanes] = (slope_ref[here, lanes] * slope).astype(BF)

        act_store(step).start()
        grad_store(step).start()

    @pl.loop(0, 4)
    def _(step):
        rows = pl.ds(pl.multiple_of(step * 512, 512), 512)
        total = dot(turned[rows, :], units[...]).astype(BF)
        up_out[pl.ds(step * 4, 4)] = total.reshape(4, 128, 1024)
        up_store(step).start()

    @pl.loop(0, 4)
    def _(step):
        lanes = pl.ds(pl.multiple_of(step * 256, 256), 256)
        total = dot_rows(act[:, lanes], cot[...]).astype(BF)
        down_out[pl.ds(step * 4, 4), :64] = total[:, :1024].reshape(4, 64, 1024)
        down_out[pl.ds(step * 4, 4), 64:] = total[:, 1024:].reshape(4, 64, 1024)
        down_store(step).start()

    for step in range(2):
        act_store(step).wait()
        grad_store(step).wait()

    @pl.loop(0, 4)
    def _(step):
        down_store(step).wait()

    @pl.loop(0, 4)
    def _(step):
        up_store(step).wait()

    ctx_store.wait()
    out_store.wait()

    @pl.loop(0, 4)
    def _(step):
        store(step).wait()


def work(odd, normed, turned, near, far, weights, bias, up_bias, cosine, sin1, sin2, segment):
    blocks = segment.reshape(2, 4, 128)
    rows = jnp.where(odd == 0, blocks, jnp.roll(blocks, 1, axis=1)).reshape(4, 1, SEQ)
    vmem, hbm = pl.BlockSpec(memory_space=pltpu.VMEM), pl.BlockSpec(memory_space=pltpu.HBM)
    table = pltpu.VMEM((TOKENS, 128), F32)
    head_b = pltpu.VMEM((2, TOKENS, 128), BF)
    head_f = pltpu.VMEM((SEQ, 128), F32)
    slab = pltpu.VMEM((16, 128, 1024), BF)
    square = pltpu.VMEM((TOKENS, 1024), BF)
    return pl.pallas_call(
        work_body,
        in_specs=[pl.BlockSpec(memory_space=pltpu.SMEM)]
        + [hbm] * 5
        + [vmem] * 2
        + [hbm] * 3
        + [vmem, hbm],
        out_specs=[hbm] * 5,
        out_shape=[
            jax.ShapeDtypeStruct((TOKENS, 4 * HD), BF),
            jax.ShapeDtypeStruct((TOKENS, 12 * HD), BF),
            jax.ShapeDtypeStruct((TOKENS, 1024), BF),
            jax.ShapeDtypeStruct((TOKENS, 1024), BF),
            jax.ShapeDtypeStruct((16, 384, 1024), BF),
        ],
        scratch_shapes=[
            table,
            table,
            table,
            pltpu.VMEM((TOKENS, 1), jnp.int32),
            pltpu.VMEM((TOKENS, D), BF),
            pltpu.VMEM((D, TOKENS), BF),
            pltpu.VMEM((TOKENS, D), BF),
            pltpu.VMEM((TOKENS, 4 * HD), BF),
            pltpu.VMEM((TOKENS, 12 * HD), BF),
            slab,
            pltpu.VMEM((256, D), BF),
            pltpu.VMEM((512, 12 * HD), F32),
            head_b,
            head_b,
            head_b,
            head_b,
            pltpu.VMEM((SEQ, SEQ), F32),
            pltpu.VMEM((2, SEQ, SEQ), F32),
            pltpu.VMEM((2, SEQ, SEQ), F32),
            pltpu.VMEM((2, SEQ, SEQ), BF),
            pltpu.VMEM((2, SEQ, SEQ), BF),
            head_f,
            head_f,
            slab,
            pltpu.SemaphoreType.DMA((13,)),
            pltpu.SemaphoreType.DMA((8,)),
            slab,
            pltpu.VMEM((16, 64, D), BF),
            square,
            square,
            pltpu.VMEM((TOKENS, 1024), F32),
            pltpu.VMEM((512, 1024), F32),
            slab,
            slab,
            pltpu.SemaphoreType.DMA((4,)),
            pltpu.SemaphoreType.DMA((4,)),
            pltpu.SemaphoreType.DMA((8,)),
            pltpu.SemaphoreType.DMA((4,)),
        ],
        compiler_params=pltpu.CompilerParams(vmem_limit_bytes=VMEM),
        cost_estimate=pl.CostEstimate(
            flops=30 << 30, bytes_accessed=64 << 20, transcendentals=2 * TOKENS * 1024
        ),
        name="work",
    )(
        odd.reshape(1), normed, turned, near, far, weights, bias, up_bias, cosine, sin1, sin2, rows,
        segment.reshape(TOKENS, 1),
    )


def branch_body(context_ref, proj_ref, act_ref, down_ref, near_ref, far_ref):
    total = dot(act_ref[...], down_ref[...].reshape(1024, 256))
    total = (total + dot(context_ref[...], proj_ref[...].reshape(256, 256))).astype(BF)
    near_ref[...] = total[:512]
    far_ref[...] = total[512:]


def branch_out(context, active, weights):
    return pl.pallas_call(
        branch_body,
        grid=(8,),
        in_specs=[
            pl.BlockSpec((TOKENS, 256), lambda n: (0, 0), pipeline_mode=pl.Buffered(1)),
            pl.BlockSpec((16, 16, 256), lambda n: (0, 16 + n, 3)),
            pl.BlockSpec((TOKENS, 1024), lambda n: (0, 0), pipeline_mode=pl.Buffered(1)),
            pl.BlockSpec((16, 64, 256), lambda n: (0, 2 + n // 4, n % 4)),
        ],
        out_specs=[pl.BlockSpec((512, 256), lambda n: (0, n))] * 2,
        out_shape=[jax.ShapeDtypeStruct((512, D), BF)] * 2,
        compiler_params=pltpu.CompilerParams(vmem_limit_bytes=VMEM),
        cost_estimate=pl.CostEstimate(
            flops=2 * TOKENS * D * 1280, bytes_accessed=12 << 20, transcendentals=0
        ),
        name="branch",
    )(context, weights, active, weights)


def pull_body(grad_ref, merged_ref, up_ref, qkv_ref, hid_near_ref, hid_far_ref, mean_ref, rstd_ref,
              near_ref, far_ref, gain_ref, shift_ref, up_ref_sum, qkv_ref_sum):
    total = dot_cols(grad_ref[...], up_ref[...].reshape(256, 1024))
    total = total + dot_cols(merged_ref[...], qkv_ref[...].reshape(256, 1024)[:, :768])
    near_ref[...] = total[:512].astype(BF)
    far_ref[...] = total[512:].astype(BF)
    hidden = jnp.concatenate([hid_near_ref[...], hid_far_ref[...]]).astype(F32)
    normal = (hidden - mean_ref[...]) * rstd_ref[...]
    gain_ref[...] = jnp.sum(total * normal, axis=0, keepdims=True)
    shift_ref[...] = jnp.sum(total, axis=0, keepdims=True)

    @pl.when(pl.program_id(0) == 0)
    def _():
        ones = jnp.ones((16, TOKENS), BF)
        up_ref_sum[...] = dot(ones, grad_ref[...])[:1]
        qkv_ref_sum[...] = dot(ones, merged_ref[...])[:1]


def pull(grad_upper, grad_merged, weights, near, far, mean, rstd):
    def whole(width):
        return pl.BlockSpec((TOKENS, width), lambda n: (0, 0), pipeline_mode=pl.Buffered(1))

    half = pl.BlockSpec((512, 256), lambda n: (0, n))
    vec = pl.BlockSpec((1, 256), lambda n: (0, n))
    return pl.pallas_call(
        pull_body,
        grid=(8,),
        in_specs=[
            whole(1024),
            whole(768),
            pl.BlockSpec((2, 128, 1024), lambda n: (n, 0, 0)),
            pl.BlockSpec((2, 128, 1024), lambda n: (n, 2, 0)),
            half,
            half,
            whole(1),
            whole(1),
        ],
        out_specs=[half] * 2
        + [vec, vec, pl.BlockSpec((1, 1024), lambda n: (0, 0)), pl.BlockSpec((1, 768), lambda n: (0, 0))],
        out_shape=[
            jax.ShapeDtypeStruct((512, D), BF),
            jax.ShapeDtypeStruct((512, D), BF),
            jax.ShapeDtypeStruct((1, D), F32),
            jax.ShapeDtypeStruct((1, D), F32),
            jax.ShapeDtypeStruct((1, 1024), F32),
            jax.ShapeDtypeStruct((1, 768), F32),
        ],
        compiler_params=pltpu.CompilerParams(vmem_limit_bytes=VMEM),
        cost_estimate=pl.CostEstimate(
            flops=2 * TOKENS * D * 1792, bytes_accessed=16 << 20, transcendentals=0
        ),
        name="pull",
    )(grad_upper, grad_merged, weights, weights, near, far, mean, rstd)


def local(
    hidden_in, norm_gain, norm_shift, qkv_weight, qkv_bias, proj_weight, proj_bias,
    up_weight, up_bias, down_weight, down_bias, segment_ids, positions, cotangent,
):
    xh, core, xl = lax.axis_index("xh"), lax.axis_index("core"), lax.axis_index("xl")
    place = 2 * xh + xl
    scalars = jnp.stack([place, core, xl]).astype(jnp.int32)
    hidden_own = hidden_in.reshape(128, D)
    cot_own = cotangent.reshape(128, D)

    parts, proj_part, down_part = deal(
        2 * xh + core, xl, up_weight, qkv_weight, proj_weight, down_weight
    )
    parts = exchange4(parts)
    proj_part = rehome(proj_part)
    proj_part = proj_part.reshape(16, 8, 256).swapaxes(0, 1).reshape(128, 256)
    send = jnp.concatenate(
        [
            parts[:, :1024],
            down_part,
            jnp.concatenate([parts[:, 1024:], proj_part], axis=1),
        ]
    )

    small = jnp.concatenate([norm_gain, norm_shift, proj_bias, down_bias, qkv_bias, up_bias])[None]
    hidden_turned = owner_order(hidden_own)
    marks = jnp.stack(
        [positions.reshape(128), lax.dynamic_slice_in_dim(segment_ids.reshape(SEQ), xl * 128, 128)]
    )
    small, hidden_turned, cot_sent, marks, send = tie(small, hidden_turned, cot_own, marks, send)
    weights = gather_plane(send)
    small = gather_step(gather_step(small, 0), 1)
    small, hidden_turned = tie(small, hidden_turned)
    hid_below, hid_above = ring_first(hidden_turned)
    small = gather_step(small, 2)
    small, hid_below, hid_above = tie(small, hid_below, hid_above)
    hid_low, hid_high = ring_second(hid_below, hid_above)
    small, hid_low, hid_high, cot_sent = tie(small, hid_low, hid_high, cot_sent)
    hid = jnp.concatenate([hidden_turned, hid_above, hid_low, hid_high, hid_below])
    hid_far = shift(hid, "core", 1)
    cot_below, cot_above = ring_first(cot_sent)
    small = gather_step(small, 3)
    small, marks, cot_below, cot_above = tie(small, marks, cot_below, cot_above)
    cot_low, cot_high = ring_second(cot_below, cot_above)
    small = gather_step(small, 4)
    small, marks, cot_low, cot_high = tie(small, marks, cot_low, cot_high)
    cot = jnp.concatenate([cot_sent, cot_above, cot_low, cot_high, cot_below])
    cot_far = shift(cot, "core", 1)
    marks = pair_gather(marks, "xl")
    small = gather_step(small, 5).astype(F32)
    marks = pair_gather(marks, "xh").reshape(4, 2, 128)
    marks = jnp.stack([pick(marks, (place + k) % 4) for k in range(4)])
    marks = jnp.stack([marks, shift(marks, "core", 1)]).transpose(2, 0, 1, 3).reshape(2, TOKENS)
    position_all, segment_all = marks[0], marks[1]

    gain = owner_order(small[:, :32].reshape(D))
    shift_row = owner_order(small[:, 32:64].reshape(D))
    out_bias = (small[:, 64:96] + small[:, 96:128]).reshape(D)
    qkv_b = small[:, 128:224].reshape(3, 2, 2, 2, 256)[:, xh, core, xl].reshape(1, 768)
    up_b = small[:, 224:352].reshape(2, 16, 2, 128)[xh, :, core]
    up_b = lax.dynamic_slice_in_dim(up_b, xl * 64, 64, 1).reshape(1, 1024)
    normed, turned, mean, rstd = norm(hid, hid_far, gain, shift_row)

    lane = jnp.arange(128) % HD
    freqs = 10000.0 ** (-(lane % 16).astype(F32) * (2.0 / ROT))
    angles = position_all.astype(F32)[:, None] * freqs
    cosine = jnp.where(lane < ROT, jnp.cos(angles), 1.0)
    sine = jnp.sin(angles)
    sin1 = jnp.where(lane < 16, sine, 0.0)
    sin2 = jnp.where((lane >= 16) & (lane < ROT), sine, 0.0)

    context, grad_merged, active, grad_upper, pack = work(
        xl, normed, turned, cot, cot_far, weights, qkv_b, up_b, cosine, sin1, sin2, segment_all
    )
    back = scatter_plane_whole(pack)

    pulled, pulled_far, gain_sum, shift_sum, up_sum, qkv_sum = pull(
        grad_upper, grad_merged, weights, hid, hid_far, mean, rstd
    )
    pulled_far = shift(pulled_far, "core", 1)
    branch, branch_far = branch_out(context, active, weights)
    gain_sum, shift_sum, up_sum, qkv_sum, branch_far, pulled_far = tie(
        gain_sum, shift_sum, up_sum, qkv_sum, branch_far, pulled_far
    )
    pulled = sum_parts(pulled, pulled_far)
    low, high = fold_first(pulled)
    branch_far = shift(branch_far, "core", 1)
    out_sum = jnp.sum(cot_own.astype(F32), axis=0)
    qkv_full = lax.dynamic_update_slice(
        jnp.zeros((3, 2, 2, 2, 256), F32), qkv_sum.reshape(3, 1, 1, 1, 256), (0, xh, core, xl, 0)
    )
    up_full = lax.dynamic_update_slice(
        jnp.zeros((2, 16, 2, 2, 64), F32), up_sum.reshape(1, 16, 1, 1, 64), (xh, 0, core, xl, 0)
    )
    sums = jnp.concatenate(
        [plain_order(s.reshape(D)).reshape(64, 32) for s in (gain_sum, shift_sum)]
        + [out_sum.reshape(64, 32), qkv_full.reshape(64, 96), up_full.reshape(64, 128)],
        axis=1,
    )
    sums = reduce_step(reduce_step(reduce_step(sums, 5), 4), 3)
    sums, branch_far, low, high = tie(sums, branch_far, low, high)
    from_below, from_above = fold_second(pulled, low, high)
    branch = sum_parts(branch, branch_far)
    low, high = fold_first(branch)
    sums = reduce_step(reduce_step(reduce_step(sums, 2), 1), 0)
    sums, low, high, from_below, from_above = tie(sums, low, high, from_below, from_above)
    branch_below, branch_above = fold_second(branch, low, high)
    sums = (sums + shift(sums, "xl", 1))[0]
    grad_own = pulled[0] + from_below.astype(F32) + from_above.astype(F32)

    own = owner_order(hidden_own).astype(F32)
    mean = jnp.mean(own, axis=-1, keepdims=True)
    centered = own - mean
    rstd = lax.rsqrt(jnp.mean(centered * centered, axis=-1, keepdims=True) + EPS)
    normal_own = centered * rstd
    scaled = grad_own * gain
    inner = jnp.mean(scaled * normal_own, axis=-1, keepdims=True)
    lifted = (scaled - jnp.mean(scaled, axis=-1, keepdims=True) - normal_own * inner) * rstd
    grad_hidden = (cot_own.astype(F32) + plain_order(lifted)).reshape(1, 128, D)

    branch = branch[0] + branch_below.astype(F32) + branch_above.astype(F32)
    block_out = hidden_own.astype(F32) + branch + out_bias
    block_out = block_out.astype(BF).reshape(1, 128, D)

    back, grad_hidden, block_out, sums = tie(back, grad_hidden, block_out, sums)
    *pieces, down_rows, proj_rows = sort(scalars, back)
    pieces = [pieces[0]] + [across(pieces[step], step) for step in (1, 2, 3)]
    proj = (rehome(proj_rows, back=True), rehome(proj_rows, back=True, other=True))
    pieces, proj = tie(pieces, proj)
    other = shift(merge(pieces), "core", 1)
    grad_up, grad_qkv, grad_down, grad_proj = spread(scalars, pieces, other, down_rows, proj)
    return (
        block_out,
        grad_hidden,
        sums[:32],
        sums[32:64],
        grad_qkv,
        sums[96:192],
        grad_proj,
        sums[64:96],
        grad_up,
        sums[192:320],
        grad_down,
        sums[64:96],
    )


def solution(mesh):
    cut = Mesh(mesh.devices.reshape(2, 4, 4, 2, 2), AXES)
    row, vec = P(SHARD, None), P(SHARD)
    tok = P(SHARD, "xl", None)
    return jax.shard_map(
        local,
        mesh=cut,
        in_specs=(
            tok, vec, vec, row, vec, row, vec, row, vec, row, vec, row, P(SHARD, "xl"), tok,
        ),
        out_specs=(tok, tok, vec, vec, row, vec, row, vec, row, vec, row, vec),
        check_vma=False,
    )
```
